32 devices in a mesh: space: 16 (over z, y, core), clus: 2 (over x).
Axes of the slice: x: 2, y: 2, z: 4, core: 2. Of those that a mesh axis runs over, the one named last changes fastest.
Arguments:
- features: bfloat16 [128, 128, 256], P('space', 'clus'), may hold values from -6 to 6
- weights: bfloat16 [16, 9, 256, 128], P('clus'), may hold values from -6 to 6
- tile_lists: int32 [16, 64], P('clus'), may hold values from 0 to 255, as said below
- labels: int32 [16, 64, 128], P('clus'), may hold values 0 or 1
Outputs:
- new_weights: bfloat16 [16, 9, 256, 128], P('clus', None, 'space')
The draws below stay inside these ranges and needn't reach their ends.
Inputs may be any that keep to these rules, and one draw needn't show every extreme that they name: `tile_lists`: counting repeats, no list names more than 8 tiles t with the same t // 16, and some list names exactly 8. `tile_lists`: for every w and g, the entries 4 * w to 4 * w + 3 of the lists of clusters 8 * g to 8 * g + 7 name, counting repeats, at most 4 tiles t with the same t // 16, and exactly 4 for some value of t // 16.
All inputs are finite; a program needn't handle non-finite values. No bound on the sum of `labels` on one device may be relied on, other than what follows from the above.
Results may differ from the reference program's by a relative error of at most 0.0037.
Values may be sent and summed in bfloat16 or wider, within the bound.
A program may use at most 128 MiB of HBM per device.

```python
import math
import jax
import jax.numpy as jnp
from jax import lax

C = 256
SPC = 128
CLUS_DEV = 8
TS = 8
ENT_DEV = 4
T_DEV = 16
CLUSTERS = 16
LIST = 64
CAP = 4
ROWS = 128
COLS = 128


def draw_tile_lists(key, part):
    bands = LIST // ENT_DEV
    group_count = CLUSTERS // CLUS_DEV
    quarter = bands // 4
    item_count = CLUS_DEV * ENT_DEV

    def one_group(group_key):
        keys = jax.random.split(group_key, 5)
        owner_perm = jax.random.permutation(keys[0], bands)
        worker_perm = jax.random.permutation(keys[1], bands)
        ranked = worker_perm[jnp.arange(bands)]
        middle = jnp.where(ranked < 2 * quarter, ranked // 2, ranked - quarter)
        base_band = owner_perm[middle]
        target_band = jax.random.randint(keys[2], (), 0, bands)
        entry_index = jnp.arange(ENT_DEV)
        first_offsets = (target_band - owner_perm[entry_index % quarter]) % bands
        used_count = jnp.sum((first_offsets[:, None] == jnp.arange(bands)[None, :]).astype(jnp.int32), axis=0)
        slot_ids = jnp.arange(bands * CAP)
        slot_value = slot_ids // CAP
        slot_level = slot_ids % CAP
        available = slot_level >= used_count[slot_value]
        preferred = slot_value == first_offsets[0]
        classes = jnp.where(available, jnp.where(preferred, 0, 1), 2)
        shuffle = jax.random.permutation(keys[3], bands * CAP)
        ordering = jnp.argsort(classes * (bands * CAP) + shuffle)
        rest_offsets = slot_value[ordering[:item_count - ENT_DEV]]
        offsets = jnp.concatenate([first_offsets, rest_offsets]).reshape(CLUS_DEV, ENT_DEV)
        owner_band = (base_band[None, :, None] + offsets[:, None, :]) % bands
        local_tile = jax.random.randint(keys[4], (CLUS_DEV, bands, ENT_DEV), 0, T_DEV)
        return (owner_band * T_DEV + local_tile).reshape(CLUS_DEV, LIST)
    group_keys = jax.random.split(jax.random.fold_in(key, 7), group_count)
    return jax.vmap(one_group)(group_keys).reshape(CLUSTERS, LIST).astype(jnp.int32)


def place_ends(entries, own_key, low, top_value):
    extent = entries.shape
    index_at = [jax.random.randint(jax.random.fold_in(own_key, axis), (), 0, extent[axis]) for axis in range(len(extent))]
    entries = entries.at[tuple(index_at)].set(low)
    longest = extent.index(max(extent))
    index_at[longest] = (index_at[longest] + 1) % extent[longest]
    return entries.at[tuple(index_at)].set(top_value)


def block_levels(stream_key, dims, shards, low, top_value):
    factor_of = 1.0
    for dim, blocks in shards:
        steps = jax.random.uniform(jax.random.fold_in(jax.random.fold_in(stream_key, 6), dim), (blocks,), jnp.float32, low / len(shards), top_value / len(shards))
        factor_of = factor_of * jnp.repeat(jnp.exp(steps), dims[dim] // blocks).reshape((-1,) + (1,) * (len(dims) - 1 - dim))
    return factor_of


def scatter_about(rng, shape, scale, reach, shards=(), held_as=jnp.bfloat16):
    array = jax.random.normal(rng, shape, jnp.float32) * scale
    if len(shards) > 0:
        array = block_levels(rng, shape, shards, -0.22, 0.18) * array
    return jnp.clip(array, min=-reach, max=reach).astype(held_as)


def setup_inputs(seed: int = 0) -> dict:
    key_of = jax.random.split(jax.random.key(seed), 5)
    features = scatter_about(key_of[0], (ROWS, COLS, C), 1.0, 6.0, ((0, 16), (1, 2)))
    weights = scatter_about(key_of[1], (CLUSTERS, 9, C, SPC), 1.0, 6.0, ((0, 2),))
    tile_lists = draw_tile_lists(jax.random.fold_in(key_of[4], 71), 0)
    labels = place_ends((jax.random.randint(key_of[3], (CLUSTERS, LIST, SPC), 0, 3) < 1).astype(jnp.int32), jax.random.fold_in(key_of[3], 1), 0, 1)
    return {"features": features, "weights": weights, "tile_lists": tile_lists, "labels": labels}


def cut_tiles(padded, tile_ids, side_cells, tile_count):
    band_index = (tile_ids // tile_count).astype(jnp.int32)
    column = (tile_ids % tile_count).astype(jnp.int32)
    anchor = jnp.zeros((), jnp.int32)

    def cut_one(row_index, col_index):
        return lax.dynamic_slice(padded, (row_index * side_cells, col_index * side_cells, anchor), (side_cells + 2, side_cells + 2, padded.shape[2]))
    return jax.vmap(cut_one)(band_index, column)

def reference(features, weights, tile_lists, labels):
    channels = features.shape[2]
    side_cells = TS
    padded = jnp.pad(features, ((1, 1), (1, 1), (0, 0)))
    scaling = 1.0 / math.sqrt(9 * channels)
    step_rate = math.sqrt(9 * channels * side_cells * side_cells / LIST)

    def one_cluster(packed):
        tile_ids, target, weight = packed
        tile_block = cut_tiles(padded, tile_ids, side_cells, T_DEV).astype(jnp.float32)
        weight_wide = weight.astype(jnp.float32)
        logits = jnp.zeros((tile_ids.shape[0], side_cells, side_cells, weight.shape[2]), jnp.float32)
        for tap_index in range(9):
            shift_row, shift_col = (tap_index // 3, tap_index % 3)
            window = tile_block[:, shift_row:shift_row + side_cells, shift_col:shift_col + side_cells, :]
            logits = logits + jnp.einsum('nabc,cs->nabs', window, weight_wide[tap_index])
        probability = jax.nn.sigmoid(logits * scaling)
        residual = (probability - target[:, None, None, :]) / (side_cells * side_cells)
        residual = lax.optimization_barrier(residual.astype(jnp.bfloat16)).astype(jnp.float32)
        pieces = []
        for tap_index in range(9):
            shift_row, shift_col = (tap_index // 3, tap_index % 3)
            window = tile_block[:, shift_row:shift_row + side_cells, shift_col:shift_col + side_cells, :]
            pieces.append(scaling * jnp.einsum('nabc,nabs->cs', window, residual))
        gradient = jnp.stack(pieces, axis=0)
        return (weight_wide - step_rate * gradient).astype(jnp.bfloat16)
    return lax.map(one_cluster, (tile_lists, labels.astype(jnp.float32), weights))
```

```python
import functools
import math

import jax
import jax.numpy as jnp
from jax import lax
from jax.experimental import pallas as pl
from jax.experimental.pallas import tpu as pltpu
from jax.sharding import PartitionSpec as P

SIDE = 8
BATCH = 4


def head_kernel(group_ref, lists_ref, map_ref, weights_ref, labels_ref, grad_ref, wide, cols, acc, chosen):
    clusters, length = lists_ref.shape
    rows_all, columns, channels = map_ref.shape
    tiles = columns // SIDE
    bands = (rows_all - 2) // SIDE
    per_group = tiles * bands
    species = weights_ref.shape[2]
    group = group_ref[0]
    scaling = 1.0 / math.sqrt(9 * channels)
    cells = SIDE * SIDE

    def widen(row, carry):
        wide[row, 1 : tiles + 1] = map_ref[row].astype(jnp.float32).reshape(tiles, SIDE, channels)
        wide[row, 0] = jnp.zeros((SIDE, channels), jnp.float32)
        wide[row, tiles + 1] = jnp.zeros((SIDE, channels), jnp.float32)
        return carry

    lax.fori_loop(0, rows_all, widen, 0)
    side_row = lax.broadcasted_iota(jnp.int32, (SIDE + 2, SIDE, channels), 1)

    def one_cluster(c, carry):
        def choose(k, count):
            chosen[count] = k
            return count + (lists_ref[c, k] // per_group == group).astype(jnp.int32)

        count = lax.fori_loop(0, length, choose, jnp.int32(0))
        acc[...] = jnp.zeros_like(acc)

        def one_batch(b, carry):
            targets = []
            for j in range(BATCH):
                slot = b * BATCH + j
                k = chosen[jnp.minimum(slot, count - 1)]
                tile = lists_ref[c, k] - group * per_group
                band, column = tile // tiles, tile % tiles
                rows = pl.ds(band * SIDE, SIDE + 2)
                left, mid, right = wide[rows, column], wide[rows, column + 1], wide[rows, column + 2]
                shifted = (
                    jnp.where(side_row == 0, pltpu.roll(left, 1, 1), pltpu.roll(mid, 1, 1)),
                    mid,
                    jnp.where(
                        side_row == SIDE - 1,
                        pltpu.roll(right, SIDE - 1, 1),
                        pltpu.roll(mid, SIDE - 1, 1),
                    ),
                )
                for dx in range(3):
                    flat = shifted[dx].reshape((SIDE + 2) * SIDE, channels)
                    for dy in range(3):
                        tap = 3 * dy + dx
                        cols[j * cells : (j + 1) * cells, tap * channels : (tap + 1) * channels] = flat[
                            dy * SIDE : dy * SIDE + cells
                        ].astype(jnp.bfloat16)
                targets.append(jnp.broadcast_to(labels_ref[c, k].astype(jnp.float32), (cells, species)))
            target = jnp.concatenate(targets, axis=0)
            logits = jnp.dot(cols[...], weights_ref[c], preferred_element_type=jnp.float32)
            probability = jax.nn.sigmoid(logits * scaling)
            slots = b * BATCH + lax.broadcasted_iota(jnp.int32, (BATCH * cells, species), 0) // cells
            residual = jnp.where(slots < count, (probability - target) * (1.0 / cells), 0.0)
            residual = residual.astype(jnp.bfloat16)
            acc[...] += lax.dot_general(
                residual, cols[...], (((0,), (0,)), ((), ())), preferred_element_type=jnp.float32
            )
            return carry

        lax.fori_loop(0, (count + BATCH - 1) // BATCH, one_batch, 0)
        for tap in range(9):
            part = slice(tap * channels, (tap + 1) * channels)
            grad_ref[c, part, :] = acc[:, part].T.astype(grad_ref.dtype)
        return carry

    lax.fori_loop(0, clusters, one_cluster, 0)


def gradient_shares(group, lists, rows, weights, labels):
    clusters, taps, channels, species = weights.shape
    rows_all, columns, _ = rows.shape
    smem = pl.BlockSpec(memory_space=pltpu.SMEM)
    vmem = pl.BlockSpec(memory_space=pltpu.VMEM)
    return pl.pallas_call(
        head_kernel,
        out_shape=jax.ShapeDtypeStruct((clusters, taps * channels, species), jnp.bfloat16),
        in_specs=[smem, smem, vmem, vmem, vmem],
        out_specs=vmem,
        scratch_shapes=[
            pltpu.VMEM((rows_all, columns // SIDE + 2, SIDE, channels), jnp.float32),
            pltpu.VMEM((BATCH * SIDE * SIDE, taps * channels), jnp.bfloat16),
            pltpu.VMEM((species, taps * channels), jnp.float32),
            pltpu.SMEM((lists.shape[1],), jnp.int32),
        ],
        compiler_params=pltpu.CompilerParams(vmem_limit_bytes=40 * 2**20),
        cost_estimate=pl.CostEstimate(flops=5 * 10**9, bytes_accessed=6 * 10**6, transcendentals=0),
    )(
        group.reshape(1),
        lists,
        rows,
        weights.reshape(clusters, taps * channels, species),
        labels.reshape(clusters, labels.shape[1], 1, species),
    )


def shards(members, features, weights, tile_lists, labels):
    spaces = lax.axis_size("space")
    position = lax.axis_index("space")
    groups = spaces // members
    group, member = position // members, position % members
    inner = [[g * members + j for j in range(members)] for g in range(groups)]
    outer = [[g * members + j for g in range(groups)] for j in range(members)]
    clusters, taps, channels, species = weights.shape
    mine = clusters // members

    rows = lax.all_gather(features, "clus", axis=1, tiled=True)
    rows = lax.all_gather(rows, "space", axis=0, tiled=True, axis_index_groups=inner)
    up = [(i, i + members) for i in range(spaces - members)]
    down = [(j, i) for i, j in up]
    before = lax.ppermute(rows[-1:], "space", up)
    after = lax.ppermute(rows[:1], "space", down)
    rows = jnp.concatenate([before, rows, after], axis=0)

    own = lambda x: lax.dynamic_slice_in_dim(x, member * mine, mine, 0)
    own_weights = own(weights)
    share = gradient_shares(group, own(tile_lists), rows, own_weights, own(labels))
    share = share.reshape(mine, taps, channels, species)
    total = lax.psum_scatter(
        share, "space", scatter_dimension=2, axis_index_groups=outer, tiled=True
    ).astype(jnp.float32)
    step = math.sqrt(9 * channels * SIDE * SIDE / tile_lists.shape[1]) / math.sqrt(9 * channels)
    depth = channels // groups
    old = lax.dynamic_slice_in_dim(own_weights, group * depth, depth, 2).astype(jnp.float32)
    new = (old - step * total).astype(jnp.bfloat16)
    return lax.all_to_all(
        new, "space", split_axis=2, concat_axis=0, axis_index_groups=inner, tiled=True
    )


def solution(mesh):
    in_specs = (
        P("space", "clus", None),
        P("clus", None, None, None),
        P("clus", None),
        P("clus", None, None),
    )
    out_specs = P("clus", None, "space", None)
    members = math.gcd(4, mesh.shape["space"])
    return jax.shard_map(
        functools.partial(shards, members),
        mesh=mesh,
        in_specs=in_specs,
        out_specs=out_specs,
        check_vma=False,
    )
```

```python
import functools
import math

import jax
import jax.numpy as jnp
from jax import lax
from jax.experimental import pallas as pl
from jax.experimental.pallas import tpu as pltpu
from jax.sharding import PartitionSpec as P

SIDE = 8
BATCH = 4


def head_kernel(group_ref, lists_ref, map_ref, weights_ref, labels_ref, grad_ref, wide, cols, acc, chosen):
    clusters, length = lists_ref.shape
    rows_all, columns, channels = map_ref.shape
    tiles = columns // SIDE
    bands = (rows_all - 2) // SIDE
    per_group = tiles * bands
    species = weights_ref.shape[2]
    group = group_ref[0]
    scaling = 1.0 / math.sqrt(9 * channels)
    cells = SIDE * SIDE

    def widen(row, carry):
        wide[row, 1 : tiles + 1] = map_ref[row].astype(jnp.float32).reshape(tiles, SIDE, channels)
        wide[row, 0] = jnp.zeros((SIDE, channels), jnp.float32)
        wide[row, tiles + 1] = jnp.zeros((SIDE, channels), jnp.float32)
        return carry

    lax.fori_loop(0, rows_all, widen, 0)
    side_row = lax.broadcasted_iota(jnp.int32, (SIDE + 2, SIDE, channels), 1)

    def one_cluster(c, carry):
        def choose(k, count):
            chosen[count] = k
            return count + (lists_ref[c, k] // per_group == group).astype(jnp.int32)

        count = lax.fori_loop(0, length, choose, jnp.int32(0))
        acc[...] = jnp.zeros_like(acc)

        def one_batch(b, carry):
            targets = []
            for j in range(BATCH):
                slot = b * BATCH + j
                k = chosen[jnp.minimum(slot, count - 1)]
                tile = lists_ref[c, k] - group * per_group
                band, column = tile // tiles, tile % tiles
                rows = pl.ds(band * SIDE, SIDE + 2)
                left, mid, right = wide[rows, column], wide[rows, column + 1], wide[rows, column + 2]
                shifted = (
                    jnp.where(side_row == 0, pltpu.roll(left, 1, 1), pltpu.roll(mid, 1, 1)),
                    mid,
                    jnp.where(
                        side_row == SIDE - 1,
                        pltpu.roll(right, SIDE - 1, 1),
                        pltpu.roll(mid, SIDE - 1, 1),
                    ),
                )
                for dx in range(3):
                    flat = shifted[dx].reshape((SIDE + 2) * SIDE, channels)
                    for dy in range(3):
                        tap = 3 * dy + dx
                        cols[j * cells : (j + 1) * cells, tap * channels : (tap + 1) * channels] = flat[
                            dy * SIDE : dy * SIDE + cells
                        ].astype(jnp.bfloat16)
                targets.append(jnp.broadcast_to(labels_ref[c, k].astype(jnp.float32), (cells, species)))
            target = jnp.concatenate(targets, axis=0)
            logits = jnp.dot(cols[...], weights_ref[c], preferred_element_type=jnp.float32)
            probability = jax.nn.sigmoid(logits * scaling)
            slots = b * BATCH + lax.broadcasted_iota(jnp.int32, (BATCH * cells, species), 0) // cells
            residual = jnp.where(slots < count, (probability - target) * (1.0 / cells), 0.0)
            residual = residual.astype(jnp.bfloat16)
            acc[...] += lax.dot_general(
                residual, cols[...], (((0,), (0,)), ((), ())), preferred_element_type=jnp.float32
            )
            return carry

        lax.fori_loop(0, (count + BATCH - 1) // BATCH, one_batch, 0)
        groups, depth = grad_ref.shape[0], grad_ref.shape[3]
        for tap in range(9):
            part = acc[:, tap * channels : (tap + 1) * channels].T.astype(grad_ref.dtype)
            grad_ref[:, c, tap] = part.reshape(groups, depth, species)
        return carry

    lax.fori_loop(0, clusters, one_cluster, 0)


def gradient_shares(groups, group, lists, rows, weights, labels):
    clusters, taps, channels, species = weights.shape
    rows_all, columns, _ = rows.shape
    smem = pl.BlockSpec(memory_space=pltpu.SMEM)
    vmem = pl.BlockSpec(memory_space=pltpu.VMEM)
    return pl.pallas_call(
        head_kernel,
        out_shape=jax.ShapeDtypeStruct(
            (groups, clusters, taps, channels // groups, species), jnp.bfloat16
        ),
        in_specs=[smem, smem, vmem, vmem, vmem],
        out_specs=vmem,
        scratch_shapes=[
            pltpu.VMEM((rows_all, columns // SIDE + 2, SIDE, channels), jnp.float32),
            pltpu.VMEM((BATCH * SIDE * SIDE, taps * channels), jnp.bfloat16),
            pltpu.VMEM((species, taps * channels), jnp.float32),
            pltpu.SMEM((lists.shape[1],), jnp.int32),
        ],
        compiler_params=pltpu.CompilerParams(vmem_limit_bytes=40 * 2**20),
        cost_estimate=pl.CostEstimate(flops=5 * 10**9, bytes_accessed=6 * 10**6, transcendentals=0),
    )(
        group.reshape(1),
        lists,
        rows,
        weights.reshape(clusters, taps * channels, species),
        labels.reshape(clusters, labels.shape[1], 1, species),
    )


def remote(src, dst, send, recv, space, clus):
    return pltpu.make_async_remote_copy(
        src_ref=src,
        dst_ref=dst,
        send_sem=send,
        recv_sem=recv,
        device_id=(space, clus),
        device_id_type=pl.DeviceIdType.MESH,
    )


def greet(space, clus):
    barrier = pltpu.get_barrier_semaphore()
    pl.semaphore_signal(
        barrier, inc=1, device_id=(space, clus), device_id_type=pl.DeviceIdType.MESH
    )


def gather_kernel(
    members, groups, sides, own_ref, rows_ref, zeros, send, passed, recv, edge_send, edge_recv, local
):
    me, side = lax.axis_index("space"), lax.axis_index("clus")
    group, member = me // members, me % members
    pair, core = member // 2, member % 2
    pairs = members // 2
    first = group * members
    sibling = first + pair * 2 + 1 - core
    width = own_ref.shape[1]
    last = rows_ref.shape[0] - 1
    offsets = [(a, b) for a in range(pairs) for b in range(sides) if (a, b) != (0, 0)]

    def spot(j, v):
        return rows_ref.at[pl.ds(1 + j * SIDE, SIDE), pl.ds(pl.multiple_of(v * width, width), width)]

    def edge(row, v):
        return rows_ref.at[pl.ds(row, 1), pl.ds(pl.multiple_of(v * width, width), width)]

    def towards(a, b):
        return first + lax.rem(pair + a, pairs) * 2 + core, lax.rem(side + b, sides)

    def origin(a, b):
        return lax.rem(pair + pairs - a, pairs) * 2 + core, lax.rem(side + sides - b, sides)

    for a, b in offsets:
        j, v = origin(a, b)
        greet(first + j, v)
    greet(sibling, side)

    @pl.when(group > 0)
    def _():
        for v in range(sides):
            greet(first - 1, v)

    @pl.when(group < groups - 1)
    def _():
        for v in range(sides):
            greet(first + members, v)

    sends_up = (member == members - 1) & (group < groups - 1)
    sends_down = (member == 0) & (group > 0)
    barrier = pltpu.get_barrier_semaphore()
    edges = (sends_up | sends_down).astype(jnp.int32) * (members * sides)
    pl.semaphore_wait(barrier, len(offsets) + 1 + edges)

    here = recv.at[member * sides + side]
    copies = []
    for i, (a, b) in enumerate(offsets):
        space, clus = towards(a, b)
        copies.append(remote(own_ref, spot(member, side), send.at[i], here, space, clus))
    copies.append(
        remote(own_ref, spot(member, side), send.at[len(offsets)], here, sibling, side)
    )
    for copy in copies:
        copy.start()
    keep = pltpu.make_async_copy(own_ref, spot(member, side), local.at[0])
    keep.start()

    def edge_copies(up):
        src = own_ref.at[pl.ds(SIDE - 1 if up else 0, 1)]
        start = first + members if up else first - members
        row, d = (0, 0) if up else (last, 1)
        return [
            remote(
                src,
                edge(row, side),
                edge_send.at[d * members * sides + j * sides + v],
                edge_recv.at[d * sides + side],
                start + j,
                v,
            )
            for j in range(members)
            for v in range(sides)
        ]

    @pl.when(sends_up)
    def _():
        for copy in edge_copies(True):
            copy.start()

    @pl.when(sends_down)
    def _():
        for copy in edge_copies(False):
            copy.start()

    zeros[...] = jnp.zeros_like(zeros)

    @pl.when(group == 0)
    def _():
        blank = pltpu.make_async_copy(zeros, rows_ref.at[pl.ds(0, 1)], local.at[1])
        blank.start()
        blank.wait()

    @pl.when(group == groups - 1)
    def _():
        blank = pltpu.make_async_copy(zeros, rows_ref.at[pl.ds(last, 1)], local.at[2])
        blank.start()
        blank.wait()

    for i, (a, b) in enumerate(offsets):
        j, v = origin(a, b)
        mark = recv.at[j * sides + v]
        block = remote(spot(j, v), spot(j, v), passed.at[i], mark, sibling, side)
        block.wait_recv()
        block.start()
        copies.append(block)
    for a in range(pairs):
        for b in range(sides):
            j, v = a * 2 + 1 - core, b
            mark = recv.at[j * sides + v]
            remote(spot(j, v), spot(j, v), passed.at[0], mark, sibling, side).wait_recv()

    @pl.when(group > 0)
    def _():
        for v in range(sides):
            remote(edge(0, v), edge(0, v), edge_send.at[0], edge_recv.at[v], sibling, side).wait_recv()

    @pl.when(group < groups - 1)
    def _():
        for v in range(sides):
            mark = edge_recv.at[sides + v]
            remote(edge(last, v), edge(last, v), edge_send.at[0], mark, sibling, side).wait_recv()

    keep.wait()
    for copy in copies:
        copy.wait_send()

    @pl.when(sends_up)
    def _():
        for copy in edge_copies(True):
            copy.wait_send()

    @pl.when(sends_down)
    def _():
        for copy in edge_copies(False):
            copy.wait_send()


def group_rows(members, groups, sides, features):
    side_rows, width, channels = features.shape
    count = members * sides
    dma = pltpu.SemaphoreType.DMA
    return pl.pallas_call(
        functools.partial(gather_kernel, members, groups, sides),
        out_shape=jax.ShapeDtypeStruct(
            (members * side_rows + 2, sides * width, channels), features.dtype
        ),
        in_specs=[pl.BlockSpec(memory_space=pl.ANY)],
        out_specs=pl.BlockSpec(memory_space=pl.ANY),
        scratch_shapes=[
            pltpu.VMEM((1, sides * width, channels), features.dtype),
            dma((count,)),
            dma((count,)),
            dma((count,)),
            dma((2 * count,)),
            dma((2 * sides,)),
            dma((3,)),
        ],
        compiler_params=pltpu.CompilerParams(collective_id=0, has_side_effects=True),
        cost_estimate=pl.CostEstimate(flops=0, bytes_accessed=4 * 10**6, transcendentals=0),
    )(features)


def reduce_kernel(
    members, groups, step, share_ref, old_ref, new_ref, landed, fresh, send, recv, out_send, out_recv, local
):
    me, side = lax.axis_index("space"), lax.axis_index("clus")
    group, member = me // members, me % members
    clusters, taps, depth, species = old_ref.shape
    piece = depth // members
    others = groups - 1

    for o in range(1, groups):
        greet(lax.rem(group + o, groups) * members + member, side)
    for o in range(1, members):
        greet(group * members + lax.rem(member + o, members), side)
    pl.semaphore_wait(pltpu.get_barrier_semaphore(), groups - 1 + members - 1)

    def part(c, o):
        to = lax.rem(group + o, groups)
        i = c * others + o - 1
        return remote(
            share_ref.at[to, c], landed.at[o - 1, c], send.at[i], recv.at[i], to * members + member, side
        )

    def handed(c, o):
        to = lax.rem(member + o, members)
        i = c * members + o
        return remote(
            fresh.at[to, c],
            new_ref.at[member * clusters + c],
            out_send.at[i],
            out_recv.at[i],
            group * members + to,
            side,
        )

    def kept(c):
        return pltpu.make_async_copy(
            fresh.at[member, c], new_ref.at[member * clusters + c], local.at[c]
        )

    for c in range(clusters):
        for o in range(1, groups):
            part(c, o).start()
    for c in range(clusters):
        for o in range(1, groups):
            part(c, o).wait_recv()

        def one_tap(tap, carry, c=c):
            total = share_ref[group, c, tap].astype(jnp.float32)
            for o in range(1, groups):
                total = total + landed[o - 1, c, tap].astype(jnp.float32)
            new = old_ref[c, tap].astype(jnp.float32) - step * total
            fresh[:, c, tap] = new.reshape(members, piece, species).astype(fresh.dtype)
            return carry

        lax.fori_loop(0, taps, one_tap, 0)
        for o in range(1, members):
            handed(c, o).start()
        kept(c).start()
    for c in range(clusters):
        kept(c).wait()
        for o in range(1, members):
            handed(c, o).wait()
        for o in range(1, groups):
            part(c, o).wait_send()


def new_shares(members, step, share, old):
    groups, clusters, taps, depth, species = share.shape
    vmem = pl.BlockSpec(memory_space=pltpu.VMEM)
    dma = pltpu.SemaphoreType.DMA
    return pl.pallas_call(
        functools.partial(reduce_kernel, members, groups, step),
        out_shape=jax.ShapeDtypeStruct(
            (members * clusters, taps, depth // members, species), old.dtype
        ),
        in_specs=[vmem, vmem],
        out_specs=vmem,
        scratch_shapes=[
            pltpu.VMEM((groups - 1, clusters, taps, depth, species), share.dtype),
            pltpu.VMEM((members, clusters, taps, depth // members, species), old.dtype),
            dma((clusters * (groups - 1),)),
            dma((clusters * (groups - 1),)),
            dma((clusters * members,)),
            dma((clusters * members,)),
            dma((clusters,)),
        ],
        compiler_params=pltpu.CompilerParams(
            collective_id=1, has_side_effects=True, vmem_limit_bytes=24 * 2**20
        ),
        cost_estimate=pl.CostEstimate(flops=10**6, bytes_accessed=4 * 10**6, transcendentals=0),
    )(share, old)


def shards(members, sides, features, weights, tile_lists, labels):
    spaces = lax.axis_size("space")
    position = lax.axis_index("space")
    groups = spaces // members
    group, member = position // members, position % members
    clusters, taps, channels, species = weights.shape
    mine = clusters // members

    rows = group_rows(members, groups, sides, features)
    own = lambda x: lax.dynamic_slice_in_dim(x, member * mine, mine, 0)
    own_weights = own(weights)
    share = gradient_shares(groups, group, own(tile_lists), rows, own_weights, own(labels))
    step = math.sqrt(9 * channels * SIDE * SIDE / tile_lists.shape[1]) / math.sqrt(9 * channels)
    depth = channels // groups
    old = lax.dynamic_slice(
        weights, (member * mine, 0, group * depth, 0), (mine, taps, depth, species)
    )
    return new_shares(members, step, share, old)


def solution(mesh):
    in_specs = (
        P("space", "clus", None),
        P("clus", None, None, None),
        P("clus", None),
        P("clus", None, None),
    )
    out_specs = P("clus", None, "space", None)
    members = 4
    return jax.shard_map(
        functools.partial(shards, members, mesh.shape["clus"]),
        mesh=mesh,
        in_specs=in_specs,
        out_specs=out_specs,
        check_vma=False,
    )
```

```python
import functools
import math

import jax
import jax.numpy as jnp
from jax import lax
from jax.experimental import pallas as pl
from jax.experimental.pallas import tpu as pltpu
from jax.sharding import PartitionSpec as P

SIDE = 8
BATCH = 4


def head_kernel(group_ref, lists_ref, map_ref, weights_ref, labels_ref, grad_ref, wide, cols, acc, chosen):
    clusters, length = lists_ref.shape
    rows_all, columns, channels = map_ref.shape
    tiles = columns // SIDE
    bands = (rows_all - 2) // SIDE
    per_group = tiles * bands
    species = weights_ref.shape[2]
    group = group_ref[0]
    scaling = 1.0 / math.sqrt(9 * channels)
    cells = SIDE * SIDE

    def widen(row, carry):
        wide[row, 1 : tiles + 1] = map_ref[row].astype(jnp.float32).reshape(tiles, SIDE, channels)
        wide[row, 0] = jnp.zeros((SIDE, channels), jnp.float32)
        wide[row, tiles + 1] = jnp.zeros((SIDE, channels), jnp.float32)
        return carry

    lax.fori_loop(0, rows_all, widen, 0)
    side_row = lax.broadcasted_iota(jnp.int32, (SIDE + 2, SIDE, channels), 1)

    def one_cluster(c, carry):
        def choose(k, count):
            chosen[count] = k
            return count + (lists_ref[c, k] // per_group == group).astype(jnp.int32)

        count = lax.fori_loop(0, length, choose, jnp.int32(0))
        acc[...] = jnp.zeros_like(acc)

        def one_batch(b, carry):
            targets = []
            for j in range(BATCH):
                slot = b * BATCH + j
                k = chosen[jnp.minimum(slot, count - 1)]
                tile = lists_ref[c, k] - group * per_group
                band, column = tile // tiles, tile % tiles
                rows = pl.ds(band * SIDE, SIDE + 2)
                left, mid, right = wide[rows, column], wide[rows, column + 1], wide[rows, column + 2]
                shifted = (
                    jnp.where(side_row == 0, pltpu.roll(left, 1, 1), pltpu.roll(mid, 1, 1)),
                    mid,
                    jnp.where(
                        side_row == SIDE - 1,
                        pltpu.roll(right, SIDE - 1, 1),
                        pltpu.roll(mid, SIDE - 1, 1),
                    ),
                )
                for dx in range(3):
                    flat = shifted[dx].reshape((SIDE + 2) * SIDE, channels)
                    for dy in range(3):
                        tap = 3 * dy + dx
                        cols[j * cells : (j + 1) * cells, tap * channels : (tap + 1) * channels] = flat[
                            dy * SIDE : dy * SIDE + cells
                        ].astype(jnp.bfloat16)
                targets.append(jnp.broadcast_to(labels_ref[c, k].astype(jnp.float32), (cells, species)))
            target = jnp.concatenate(targets, axis=0)
            logits = jnp.dot(cols[...], weights_ref[c], preferred_element_type=jnp.float32)
            probability = jax.nn.sigmoid(logits * scaling)
            slots = b * BATCH + lax.broadcasted_iota(jnp.int32, (BATCH * cells, species), 0) // cells
            residual = jnp.where(slots < count, (probability - target) * (1.0 / cells), 0.0)
            residual = residual.astype(jnp.bfloat16)
            acc[...] += lax.dot_general(
                residual, cols[...], (((0,), (0,)), ((), ())), preferred_element_type=jnp.float32
            )
            return carry

        lax.fori_loop(0, (count + BATCH - 1) // BATCH, one_batch, 0)
        groups, depth = grad_ref.shape[0], grad_ref.shape[3]
        for tap in range(9):
            part = acc[:, tap * channels : (tap + 1) * channels].T.astype(grad_ref.dtype)
            grad_ref[:, c, tap] = part.reshape(groups, depth, species)
        return carry

    lax.fori_loop(0, clusters, one_cluster, 0)


def gradient_shares(groups, group, lists, rows, weights, labels):
    clusters, taps, channels, species = weights.shape
    rows_all, columns, _ = rows.shape
    smem = pl.BlockSpec(memory_space=pltpu.SMEM)
    vmem = pl.BlockSpec(memory_space=pltpu.VMEM)
    return pl.pallas_call(
        head_kernel,
        out_shape=jax.ShapeDtypeStruct(
            (groups, clusters, taps, channels // groups, species), jnp.bfloat16
        ),
        in_specs=[smem, smem, vmem, vmem, vmem],
        out_specs=vmem,
        scratch_shapes=[
            pltpu.VMEM((rows_all, columns // SIDE + 2, SIDE, channels), jnp.float32),
            pltpu.VMEM((BATCH * SIDE * SIDE, taps * channels), jnp.bfloat16),
            pltpu.VMEM((species, taps * channels), jnp.float32),
            pltpu.SMEM((lists.shape[1],), jnp.int32),
        ],
        compiler_params=pltpu.CompilerParams(vmem_limit_bytes=40 * 2**20),
        cost_estimate=pl.CostEstimate(flops=5 * 10**9, bytes_accessed=6 * 10**6, transcendentals=0),
    )(
        group.reshape(1),
        lists,
        rows,
        weights.reshape(clusters, taps * channels, species),
        labels.reshape(clusters, labels.shape[1], 1, species),
    )


def remote(src, dst, send, recv, space, clus):
    return pltpu.make_async_remote_copy(
        src_ref=src,
        dst_ref=dst,
        send_sem=send,
        recv_sem=recv,
        device_id=(space, clus),
        device_id_type=pl.DeviceIdType.MESH,
    )


def greet(space, clus):
    barrier = pltpu.get_barrier_semaphore()
    pl.semaphore_signal(
        barrier, inc=1, device_id=(space, clus), device_id_type=pl.DeviceIdType.MESH
    )


def gather_kernel(
    members, groups, sides, own_ref, rows_ref, zeros, send, passed, recv, edge_send, edge_recv, local
):
    me, side = lax.axis_index("space"), lax.axis_index("clus")
    group, member = me // members, me % members
    pair, core = member // 2, member % 2
    pairs = members // 2
    first = group * members
    sibling = first + pair * 2 + 1 - core
    width = own_ref.shape[1]
    last = rows_ref.shape[0] - 1
    offsets = [(a, b) for a in range(pairs) for b in range(sides) if (a, b) != (0, 0)]

    def spot(j, v):
        return rows_ref.at[pl.ds(1 + j * SIDE, SIDE), pl.ds(pl.multiple_of(v * width, width), width)]

    def edge(row, v):
        return rows_ref.at[pl.ds(row, 1), pl.ds(pl.multiple_of(v * width, width), width)]

    def towards(a, b):
        return first + lax.rem(pair + a, pairs) * 2 + core, lax.rem(side + b, sides)

    def origin(a, b):
        return lax.rem(pair + pairs - a, pairs) * 2 + core, lax.rem(side + sides - b, sides)

    for a, b in offsets:
        j, v = origin(a, b)
        greet(first + j, v)
    greet(sibling, side)

    @pl.when(group > 0)
    def _():
        for v in range(sides):
            greet(first - 1, v)

    @pl.when(group < groups - 1)
    def _():
        for v in range(sides):
            greet(first + members, v)

    sends_up = (member == members - 1) & (group < groups - 1)
    sends_down = (member == 0) & (group > 0)
    barrier = pltpu.get_barrier_semaphore()
    edges = (sends_up | sends_down).astype(jnp.int32) * (members * sides)
    pl.semaphore_wait(barrier, len(offsets) + 1 + edges)

    here = recv.at[member * sides + side]
    copies = []
    for i, (a, b) in enumerate(offsets):
        space, clus = towards(a, b)
        copies.append(remote(own_ref, spot(member, side), send.at[i], here, space, clus))
    copies.append(
        remote(own_ref, spot(member, side), send.at[len(offsets)], here, sibling, side)
    )
    for copy in copies:
        copy.start()
    keep = pltpu.make_async_copy(own_ref, spot(member, side), local.at[0])
    keep.start()

    def edge_copies(up):
        src = own_ref.at[pl.ds(SIDE - 1 if up else 0, 1)]
        start = first + members if up else first - members
        row, d = (0, 0) if up else (last, 1)
        return [
            remote(
                src,
                edge(row, side),
                edge_send.at[d * members * sides + j * sides + v],
                edge_recv.at[d * sides + side],
                start + j,
                v,
            )
            for j in range(members)
            for v in range(sides)
        ]

    @pl.when(sends_up)
    def _():
        for copy in edge_copies(True):
            copy.start()

    @pl.when(sends_down)
    def _():
        for copy in edge_copies(False):
            copy.start()

    zeros[...] = jnp.zeros_like(zeros)

    @pl.when(group == 0)
    def _():
        blank = pltpu.make_async_copy(zeros, rows_ref.at[pl.ds(0, 1)], local.at[1])
        blank.start()
        blank.wait()

    @pl.when(group == groups - 1)
    def _():
        blank = pltpu.make_async_copy(zeros, rows_ref.at[pl.ds(last, 1)], local.at[2])
        blank.start()
        blank.wait()

    for i, (a, b) in enumerate(offsets):
        j, v = origin(a, b)
        mark = recv.at[j * sides + v]
        block = remote(spot(j, v), spot(j, v), passed.at[i], mark, sibling, side)
        block.wait_recv()
        block.start()
        copies.append(block)
    for a in range(pairs):
        for b in range(sides):
            j, v = a * 2 + 1 - core, b
            mark = recv.at[j * sides + v]
            remote(spot(j, v), spot(j, v), passed.at[0], mark, sibling, side).wait_recv()

    @pl.when(group > 0)
    def _():
        for v in range(sides):
            remote(edge(0, v), edge(0, v), edge_send.at[0], edge_recv.at[v], sibling, side).wait_recv()

    @pl.when(group < groups - 1)
    def _():
        for v in range(sides):
            mark = edge_recv.at[sides + v]
            remote(edge(last, v), edge(last, v), edge_send.at[0], mark, sibling, side).wait_recv()

    keep.wait()
    for copy in copies:
        copy.wait_send()

    @pl.when(sends_up)
    def _():
        for copy in edge_copies(True):
            copy.wait_send()

    @pl.when(sends_down)
    def _():
        for copy in edge_copies(False):
            copy.wait_send()


def group_rows(members, groups, sides, features):
    side_rows, width, channels = features.shape
    count = members * sides
    dma = pltpu.SemaphoreType.DMA
    return pl.pallas_call(
        functools.partial(gather_kernel, members, groups, sides),
        out_shape=jax.ShapeDtypeStruct(
            (members * side_rows + 2, sides * width, channels), features.dtype
        ),
        in_specs=[pl.BlockSpec(memory_space=pl.ANY)],
        out_specs=pl.BlockSpec(memory_space=pl.ANY),
        scratch_shapes=[
            pltpu.VMEM((1, sides * width, channels), features.dtype),
            dma((count,)),
            dma((count,)),
            dma((count,)),
            dma((2 * count,)),
            dma((2 * sides,)),
            dma((3,)),
        ],
        compiler_params=pltpu.CompilerParams(collective_id=0, has_side_effects=True),
        cost_estimate=pl.CostEstimate(flops=0, bytes_accessed=4 * 10**6, transcendentals=0),
    )(features)


def reduce_kernel(
    members,
    groups,
    step,
    share_ref,
    weights_ref,
    new_ref,
    old,
    near,
    relay,
    joined,
    far,
    fresh,
    near_send,
    near_recv,
    relay_send,
    relay_recv,
    far_send,
    far_recv,
    out_send,
    out_recv,
    local,
):
    me, side = lax.axis_index("space"), lax.axis_index("clus")
    group, member = me // members, me % members
    clusters, taps, depth, species = old.shape
    piece = depth // members
    pairs = groups // 2
    pair = group // 2

    def joint_of(p):
        return p * 2 + (p < pairs // 2).astype(jnp.int32)

    def at(g):
        return g * members + member

    partner = pair * 2 + 1 - group % 2
    is_joint = group == joint_of(pair)
    not_joint = group != joint_of(pair)

    kept_weights = pltpu.make_async_copy(
        weights_ref.at[
            pl.ds(member * clusters, clusters),
            :,
            pl.ds(pl.multiple_of(group * depth, depth), depth),
        ],
        old,
        local.at[clusters],
    )
    kept_weights.start()

    greet(at(partner), side)
    for q in range(1, pairs):
        greet(at(joint_of(lax.rem(pair + q, pairs))), side)
    for o in range(1, members):
        greet(group * members + lax.rem(member + o, members), side)
    pl.semaphore_wait(
        pltpu.get_barrier_semaphore(), members + is_joint.astype(jnp.int32) * (2 * (pairs - 1))
    )

    parts = [(c, q, e) for c in range(clusters) for q in range(1, pairs) for e in range(2)]

    def index(c, q, e):
        return (c * (pairs - 1) + q - 1) * 2 + e

    def to_partner(c):
        return remote(
            share_ref.at[partner, c], near.at[c], near_send.at[c], near_recv.at[c], at(partner), side
        )

    def to_joint(c, q, e):
        i = index(c, q, e)
        return remote(
            share_ref.at[lax.rem(pair + q, pairs) * 2 + e, c],
            relay.at[i],
            relay_send.at[i],
            relay_recv.at[i],
            at(partner),
            side,
        )

    def across(c, q, e):
        i = index(c, q, e)
        j = c * (pairs - 1) + q - 1
        to = lax.rem(pair + q, pairs) * 2 + e
        return remote(joined.at[i], far.at[j], far_send.at[i], far_recv.at[j], at(to), side)

    def handed(c, o):
        to = lax.rem(member + o, members)
        i = c * members + o
        return remote(
            fresh.at[to, c],
            new_ref.at[member * clusters + c],
            out_send.at[i],
            out_recv.at[i],
            group * members + to,
            side,
        )

    def kept(c):
        return pltpu.make_async_copy(
            fresh.at[member, c], new_ref.at[member * clusters + c], local.at[c]
        )

    @pl.when(not_joint)
    def _():
        for c, q, e in parts:
            to_joint(c, q, e).start()

    for c in range(clusters):
        to_partner(c).start()

    @pl.when(is_joint)
    def _():
        for c, q, e in parts:
            to_joint(c, q, e).wait_recv()
            i, to = index(c, q, e), lax.rem(pair + q, pairs) * 2 + e

            def join(tap, carry, i=i, to=to, c=c):
                total = share_ref[to, c, tap].astype(jnp.float32) + relay[i, tap].astype(jnp.float32)
                joined[i, tap] = total.astype(joined.dtype)
                return carry

            lax.fori_loop(0, taps, join, 0)
            across(c, q, e).start()

    kept_weights.wait()
    for c in range(clusters):
        to_partner(c).wait_recv()
        for q in range(1, pairs):
            across(c, q, 0).wait_recv()

        def one_tap(tap, carry, c=c):
            total = share_ref[group, c, tap].astype(jnp.float32) + near[c, tap].astype(jnp.float32)
            for q in range(1, pairs):
                total = total + far[c * (pairs - 1) + q - 1, tap].astype(jnp.float32)
            new = old[c, tap].astype(jnp.float32) - step * total
            fresh[:, c, tap] = new.reshape(members, piece, species).astype(fresh.dtype)
            return carry

        lax.fori_loop(0, taps, one_tap, 0)
        for o in range(1, members):
            handed(c, o).start()
        kept(c).start()
    for c in range(clusters):
        kept(c).wait()
        for o in range(1, members):
            handed(c, o).wait()
        to_partner(c).wait_send()

    @pl.when(not_joint)
    def _():
        for c, q, e in parts:
            to_joint(c, q, e).wait_send()

    @pl.when(is_joint)
    def _():
        for c, q, e in parts:
            across(c, q, e).wait_send()


def new_shares(members, step, share, weights):
    groups, clusters, taps, depth, species = share.shape
    away = clusters * (groups // 2 - 1)
    block = (taps, depth, species)
    dma = pltpu.SemaphoreType.DMA
    vmem = pl.BlockSpec(memory_space=pltpu.VMEM)
    return pl.pallas_call(
        functools.partial(reduce_kernel, members, groups, step),
        out_shape=jax.ShapeDtypeStruct(
            (members * clusters, taps, depth // members, species), weights.dtype
        ),
        in_specs=[vmem, pl.BlockSpec(memory_space=pl.ANY)],
        out_specs=vmem,
        scratch_shapes=[
            pltpu.VMEM((clusters,) + block, weights.dtype),
            pltpu.VMEM((clusters,) + block, share.dtype),
            pltpu.VMEM((2 * away,) + block, share.dtype),
            pltpu.VMEM((2 * away,) + block, share.dtype),
            pltpu.VMEM((away,) + block, share.dtype),
            pltpu.VMEM((members, clusters, taps, depth // members, species), weights.dtype),
            dma((clusters,)),
            dma((clusters,)),
            dma((2 * away,)),
            dma((2 * away,)),
            dma((2 * away,)),
            dma((away,)),
            dma((clusters * members,)),
            dma((clusters * members,)),
            dma((clusters + 1,)),
        ],
        compiler_params=pltpu.CompilerParams(
            collective_id=1, has_side_effects=True, vmem_limit_bytes=24 * 2**20
        ),
        cost_estimate=pl.CostEstimate(flops=10**6, bytes_accessed=4 * 10**6, transcendentals=0),
    )(share, weights)


def shards(members, sides, features, weights, tile_lists, labels):
    spaces = lax.axis_size("space")
    position = lax.axis_index("space")
    groups = spaces // members
    group, member = position // members, position % members
    clusters, taps, channels, species = weights.shape
    mine = clusters // members

    rows = group_rows(members, groups, sides, features)
    own = lambda x: lax.dynamic_slice_in_dim(x, member * mine, mine, 0)
    own_weights = own(weights)
    share = gradient_shares(groups, group, own(tile_lists), rows, own_weights, own(labels))
    step = math.sqrt(9 * channels * SIDE * SIDE / tile_lists.shape[1]) / math.sqrt(9 * channels)
    return new_shares(members, step, share, weights)


def solution(mesh):
    in_specs = (
        P("space", "clus", None),
        P("clus", None, None, None),
        P("clus", None),
        P("clus", None, None),
    )
    out_specs = P("clus", None, "space", None)
    members = 4
    return jax.shard_map(
        functools.partial(shards, members, mesh.shape["clus"]),
        mesh=mesh,
        in_specs=in_specs,
        out_specs=out_specs,
        check_vma=False,
    )
```

```python
import functools
import math

import jax
import jax.numpy as jnp
from jax import lax
from jax.experimental import pallas as pl
from jax.experimental.pallas import tpu as pltpu
from jax.sharding import PartitionSpec as P

SIDE = 8
BATCH = 4


def head_kernel(
    members, lists_ref, map_ref, weights_all, labels_all, grad_ref, wide, cols, acc, chosen, weights_ref, labels_ref, sems
):
    me = lax.axis_index("space")
    group, member = me // members, me % members
    clusters, length = labels_ref.shape[0], labels_ref.shape[1]
    mine = pl.ds(member * clusters, clusters)
    fetches = [
        pltpu.make_async_copy(weights_all.at[mine], weights_ref, sems.at[0]),
        pltpu.make_async_copy(labels_all.at[mine], labels_ref, sems.at[1]),
    ]
    for fetch in fetches:
        fetch.start()
    rows_all, columns, channels = map_ref.shape
    tiles = columns // SIDE
    bands = (rows_all - 2) // SIDE
    per_group = tiles * bands
    species = weights_ref.shape[2]
    scaling = 1.0 / math.sqrt(9 * channels)
    cells = SIDE * SIDE

    def widen(row, carry):
        wide[row, 1 : tiles + 1] = map_ref[row].astype(jnp.float32).reshape(tiles, SIDE, channels)
        wide[row, 0] = jnp.zeros((SIDE, channels), jnp.float32)
        wide[row, tiles + 1] = jnp.zeros((SIDE, channels), jnp.float32)
        return carry

    lax.fori_loop(0, rows_all, widen, 0)
    for fetch in fetches:
        fetch.wait()
    side_row = lax.broadcasted_iota(jnp.int32, (SIDE + 2, SIDE, channels), 1)

    def one_cluster(c, carry):
        def choose(k, count):
            chosen[count] = k
            return count + (lists_ref[member * clusters + c, k] // per_group == group).astype(jnp.int32)

        count = lax.fori_loop(0, length, choose, jnp.int32(0))
        acc[...] = jnp.zeros_like(acc)

        def one_batch(b, carry):
            targets = []
            for j in range(BATCH):
                slot = b * BATCH + j
                k = chosen[jnp.minimum(slot, count - 1)]
                tile = lists_ref[member * clusters + c, k] - group * per_group
                band, column = tile // tiles, tile % tiles
                rows = pl.ds(band * SIDE, SIDE + 2)
                left, mid, right = wide[rows, column], wide[rows, column + 1], wide[rows, column + 2]
                shifted = (
                    jnp.where(side_row == 0, pltpu.roll(left, 1, 1), pltpu.roll(mid, 1, 1)),
                    mid,
                    jnp.where(
                        side_row == SIDE - 1,
                        pltpu.roll(right, SIDE - 1, 1),
                        pltpu.roll(mid, SIDE - 1, 1),
                    ),
                )
                for dx in range(3):
                    flat = shifted[dx].reshape((SIDE + 2) * SIDE, channels)
                    for dy in range(3):
                        tap = 3 * dy + dx
                        cols[j * cells : (j + 1) * cells, tap * channels : (tap + 1) * channels] = flat[
                            dy * SIDE : dy * SIDE + cells
                        ].astype(jnp.bfloat16)
                targets.append(jnp.broadcast_to(labels_ref[c, pl.ds(k, 1), :].astype(jnp.float32), (cells, species)))
            target = jnp.concatenate(targets, axis=0)
            logits = jnp.dot(cols[...], weights_ref[c], preferred_element_type=jnp.float32)
            probability = jax.nn.sigmoid(logits * scaling)
            slots = b * BATCH + lax.broadcasted_iota(jnp.int32, (BATCH * cells, species), 0) // cells
            residual = jnp.where(slots < count, (probability - target) * (1.0 / cells), 0.0)
            residual = residual.astype(jnp.bfloat16)
            acc[...] += lax.dot_general(
                residual, cols[...], (((0,), (0,)), ((), ())), preferred_element_type=jnp.float32
            )
            return carry

        lax.fori_loop(0, (count + BATCH - 1) // BATCH, one_batch, 0)
        groups, depth = grad_ref.shape[0], grad_ref.shape[3]
        for tap in range(9):
            part = acc[:, tap * channels : (tap + 1) * channels].T.astype(grad_ref.dtype)
            grad_ref[:, c, tap] = part.reshape(groups, depth, species)
        return carry

    lax.fori_loop(0, clusters, one_cluster, 0)


def gradient_shares(members, groups, lists, rows, weights, labels):
    count, taps, channels, species = weights.shape
    rows_all, columns, _ = rows.shape
    clusters = count // members
    smem = pl.BlockSpec(memory_space=pltpu.SMEM)
    vmem = pl.BlockSpec(memory_space=pltpu.VMEM)
    whole = pl.BlockSpec(memory_space=pl.ANY)
    return pl.pallas_call(
        functools.partial(head_kernel, members),
        out_shape=jax.ShapeDtypeStruct(
            (groups, clusters, taps, channels // groups, species), jnp.bfloat16
        ),
        in_specs=[smem, vmem, whole, whole],
        out_specs=vmem,
        scratch_shapes=[
            pltpu.VMEM((rows_all, columns // SIDE + 2, SIDE, channels), jnp.float32),
            pltpu.VMEM((BATCH * SIDE * SIDE, taps * channels), jnp.bfloat16),
            pltpu.VMEM((species, taps * channels), jnp.float32),
            pltpu.SMEM((lists.shape[1],), jnp.int32),
            pltpu.VMEM((clusters, taps * channels, species), weights.dtype),
            pltpu.VMEM((clusters,) + labels.shape[1:], labels.dtype),
            pltpu.SemaphoreType.DMA((2,)),
        ],
        compiler_params=pltpu.CompilerParams(vmem_limit_bytes=40 * 2**20),
        cost_estimate=pl.CostEstimate(flops=5 * 10**9, bytes_accessed=6 * 10**6, transcendentals=0),
    )(lists, rows, weights.reshape(count, taps * channels, species), labels)


def remote(src, dst, send, recv, space, clus):
    return pltpu.make_async_remote_copy(
        src_ref=src,
        dst_ref=dst,
        send_sem=send,
        recv_sem=recv,
        device_id=(space, clus),
        device_id_type=pl.DeviceIdType.MESH,
    )


def greet(space, clus):
    barrier = pltpu.get_barrier_semaphore()
    pl.semaphore_signal(
        barrier, inc=1, device_id=(space, clus), device_id_type=pl.DeviceIdType.MESH
    )


def gather_kernel(
    members, groups, sides, own_ref, rows_ref, send, passed, recv, edge_send, edge_recv, local
):
    me, side = lax.axis_index("space"), lax.axis_index("clus")
    group, member = me // members, me % members
    pair, core = member // 2, member % 2
    pairs = members // 2
    first = group * members
    sibling = first + pair * 2 + 1 - core
    width = own_ref.shape[1]
    last = rows_ref.shape[0] - 1
    offsets = [(a, b) for a in range(pairs) for b in range(sides) if (a, b) != (0, 0)]

    def spot(j, v):
        return rows_ref.at[pl.ds(1 + j * SIDE, SIDE), pl.ds(pl.multiple_of(v * width, width), width)]

    def edge(row, v):
        return rows_ref.at[pl.ds(row, 1), pl.ds(pl.multiple_of(v * width, width), width)]

    def towards(a, b):
        return first + lax.rem(pair + a, pairs) * 2 + core, lax.rem(side + b, sides)

    def origin(a, b):
        return lax.rem(pair + pairs - a, pairs) * 2 + core, lax.rem(side + sides - b, sides)

    for a, b in offsets:
        j, v = origin(a, b)
        greet(first + j, v)
    greet(sibling, side)

    @pl.when(group > 0)
    def _():
        for v in range(sides):
            greet(first - 1, v)

    @pl.when(group < groups - 1)
    def _():
        for v in range(sides):
            greet(first + members, v)

    sends_up = (member == members - 1) & (group < groups - 1)
    sends_down = (member == 0) & (group > 0)
    barrier = pltpu.get_barrier_semaphore()
    edges = (sends_up | sends_down).astype(jnp.int32) * (members * sides)
    pl.semaphore_wait(barrier, len(offsets) + 1 + edges)

    here = recv.at[member * sides + side]
    copies = []
    for i, (a, b) in enumerate(offsets):
        space, clus = towards(a, b)
        copies.append(remote(own_ref, spot(member, side), send.at[i], here, space, clus))
    copies.append(
        remote(own_ref, spot(member, side), send.at[len(offsets)], here, sibling, side)
    )
    def edge_copies(up):
        src = own_ref.at[pl.ds(SIDE - 1 if up else 0, 1)]
        start = first + members if up else first - members
        row, d = (0, 0) if up else (last, 1)
        return [
            remote(
                src,
                edge(row, side),
                edge_send.at[d * members * sides + j * sides + v],
                edge_recv.at[d * sides + side],
                start + j,
                v,
            )
            for j in range(members)
            for v in range(sides)
        ]

    @pl.when(sends_up)
    def _():
        for copy in edge_copies(True):
            copy.start()

    @pl.when(sends_down)
    def _():
        for copy in edge_copies(False):
            copy.start()

    for copy in copies:
        copy.start()
    keep = pltpu.make_async_copy(own_ref, spot(member, side), local.at[0])
    keep.start()

    @pl.when(group == 0)
    def _():
        rows_ref[0] = jnp.zeros_like(rows_ref[0])

    @pl.when(group == groups - 1)
    def _():
        rows_ref[last] = jnp.zeros_like(rows_ref[last])

    for i, (a, b) in enumerate(offsets):
        j, v = origin(a, b)
        mark = recv.at[j * sides + v]
        block = remote(spot(j, v), spot(j, v), passed.at[i], mark, sibling, side)
        block.wait_recv()
        block.start()
        copies.append(block)
    for a in range(pairs):
        for b in range(sides):
            j, v = a * 2 + 1 - core, b
            mark = recv.at[j * sides + v]
            remote(spot(j, v), spot(j, v), passed.at[0], mark, sibling, side).wait_recv()

    @pl.when(group > 0)
    def _():
        for v in range(sides):
            remote(edge(0, v), edge(0, v), edge_send.at[0], edge_recv.at[v], sibling, side).wait_recv()

    @pl.when(group < groups - 1)
    def _():
        for v in range(sides):
            mark = edge_recv.at[sides + v]
            remote(edge(last, v), edge(last, v), edge_send.at[0], mark, sibling, side).wait_recv()

    keep.wait()
    for copy in copies:
        copy.wait_send()

    @pl.when(sends_up)
    def _():
        for copy in edge_copies(True):
            copy.wait_send()

    @pl.when(sends_down)
    def _():
        for copy in edge_copies(False):
            copy.wait_send()


def group_rows(members, groups, sides, features):
    side_rows, width, channels = features.shape
    count = members * sides
    dma = pltpu.SemaphoreType.DMA
    return pl.pallas_call(
        functools.partial(gather_kernel, members, groups, sides),
        out_shape=jax.ShapeDtypeStruct(
            (members * side_rows + 2, sides * width, channels), features.dtype
        ),
        in_specs=[pl.BlockSpec(memory_space=pl.ANY)],
        out_specs=pl.BlockSpec(memory_space=pltpu.VMEM),
        scratch_shapes=[
            dma((count,)),
            dma((count,)),
            dma((count,)),
            dma((2 * count,)),
            dma((2 * sides,)),
            dma((1,)),
        ],
        compiler_params=pltpu.CompilerParams(
            collective_id=0, has_side_effects=True, vmem_limit_bytes=16 * 2**20
        ),
        cost_estimate=pl.CostEstimate(flops=0, bytes_accessed=4 * 10**6, transcendentals=0),
    )(features)


def reduce_kernel(
    members,
    groups,
    step,
    share_ref,
    weights_ref,
    new_ref,
    old,
    near,
    relay,
    joined,
    far,
    fresh,
    near_send,
    near_recv,
    relay_send,
    relay_recv,
    far_send,
    far_recv,
    out_send,
    out_recv,
    local,
):
    me, side = lax.axis_index("space"), lax.axis_index("clus")
    group, member = me // members, me % members
    clusters, taps, depth, species = old.shape
    piece = depth // members
    pairs = groups // 2
    pair = group // 2

    def joint_of(p):
        return p * 2 + (p < pairs // 2).astype(jnp.int32)

    def at(g):
        return g * members + member

    partner = pair * 2 + 1 - group % 2
    is_joint = group == joint_of(pair)
    not_joint = group != joint_of(pair)

    kept_weights = pltpu.make_async_copy(
        weights_ref.at[
            pl.ds(member * clusters, clusters),
            :,
            pl.ds(pl.multiple_of(group * depth, depth), depth),
        ],
        old,
        local.at[clusters],
    )
    kept_weights.start()

    greet(at(partner), side)
    for q in range(1, pairs):
        greet(at(joint_of(lax.rem(pair + q, pairs))), side)
    for o in range(1, members):
        greet(group * members + lax.rem(member + o, members), side)
    pl.semaphore_wait(
        pltpu.get_barrier_semaphore(), members + is_joint.astype(jnp.int32) * (2 * (pairs - 1))
    )

    parts = [(c, q, e) for c in range(clusters) for q in range(1, pairs) for e in range(2)]

    def index(c, q, e):
        return (c * (pairs - 1) + q - 1) * 2 + e

    def to_partner(c):
        return remote(
            share_ref.at[partner, c], near.at[c], near_send.at[c], near_recv.at[c], at(partner), side
        )

    def to_joint(c, q, e):
        i = index(c, q, e)
        return remote(
            share_ref.at[lax.rem(pair + q, pairs) * 2 + e, c],
            relay.at[i],
            relay_send.at[i],
            relay_recv.at[i],
            at(partner),
            side,
        )

    def across(c, q, e):
        i = index(c, q, e)
        j = c * (pairs - 1) + q - 1
        to = lax.rem(pair + q, pairs) * 2 + e
        return remote(joined.at[i], far.at[j], far_send.at[i], far_recv.at[j], at(to), side)

    def handed(c, o):
        to = lax.rem(member + o, members)
        i = c * members + o
        return remote(
            fresh.at[to, c],
            new_ref.at[member * clusters + c],
            out_send.at[i],
            out_recv.at[i],
            group * members + to,
            side,
        )

    def kept(c):
        return pltpu.make_async_copy(
            fresh.at[member, c], new_ref.at[member * clusters + c], local.at[c]
        )

    @pl.when(not_joint)
    def _():
        for c, q, e in parts:
            to_joint(c, q, e).start()

    for c in range(clusters):
        to_partner(c).start()

    @pl.when(is_joint)
    def _():
        for c, q, e in parts:
            to_joint(c, q, e).wait_recv()
            i, to = index(c, q, e), lax.rem(pair + q, pairs) * 2 + e

            def join(tap, carry, i=i, to=to, c=c):
                total = share_ref[to, c, tap].astype(jnp.float32) + relay[i, tap].astype(jnp.float32)
                joined[i, tap] = total.astype(joined.dtype)
                return carry

            lax.fori_loop(0, taps, join, 0)
            across(c, q, e).start()

    kept_weights.wait()
    for c in range(clusters):
        to_partner(c).wait_recv()
        for q in range(1, pairs):
            across(c, q, 0).wait_recv()

        def one_tap(tap, carry, c=c):
            total = share_ref[group, c, tap].astype(jnp.float32) + near[c, tap].astype(jnp.float32)
            for q in range(1, pairs):
                total = total + far[c * (pairs - 1) + q - 1, tap].astype(jnp.float32)
            new = old[c, tap].astype(jnp.float32) - step * total
            fresh[:, c, tap] = new.reshape(members, piece, species).astype(fresh.dtype)
            return carry

        lax.fori_loop(0, taps, one_tap, 0)
        for o in range(1, members):
            handed(c, o).start()
        kept(c).start()
    for c in range(clusters):
        kept(c).wait()
        for o in range(1, members):
            handed(c, o).wait()
        to_partner(c).wait_send()

    @pl.when(not_joint)
    def _():
        for c, q, e in parts:
            to_joint(c, q, e).wait_send()

    @pl.when(is_joint)
    def _():
        for c, q, e in parts:
            across(c, q, e).wait_send()


def new_shares(members, step, share, weights):
    groups, clusters, taps, depth, species = share.shape
    away = clusters * (groups // 2 - 1)
    block = (taps, depth, species)
    dma = pltpu.SemaphoreType.DMA
    vmem = pl.BlockSpec(memory_space=pltpu.VMEM)
    return pl.pallas_call(
        functools.partial(reduce_kernel, members, groups, step),
        out_shape=jax.ShapeDtypeStruct(
            (members * clusters, taps, depth // members, species), weights.dtype
        ),
        in_specs=[vmem, pl.BlockSpec(memory_space=pl.ANY)],
        out_specs=vmem,
        scratch_shapes=[
            pltpu.VMEM((clusters,) + block, weights.dtype),
            pltpu.VMEM((clusters,) + block, share.dtype),
            pltpu.VMEM((2 * away,) + block, share.dtype),
            pltpu.VMEM((2 * away,) + block, share.dtype),
            pltpu.VMEM((away,) + block, share.dtype),
            pltpu.VMEM((members, clusters, taps, depth // members, species), weights.dtype),
            dma((clusters,)),
            dma((clusters,)),
            dma((2 * away,)),
            dma((2 * away,)),
            dma((2 * away,)),
            dma((away,)),
            dma((clusters * members,)),
            dma((clusters * members,)),
            dma((clusters + 1,)),
        ],
        compiler_params=pltpu.CompilerParams(
            collective_id=1, has_side_effects=True, vmem_limit_bytes=24 * 2**20
        ),
        cost_estimate=pl.CostEstimate(flops=10**6, bytes_accessed=4 * 10**6, transcendentals=0),
    )(share, weights)


def shards(members, sides, features, weights, tile_lists, labels):
    groups = lax.axis_size("space") // members
    channels = weights.shape[2]
    rows = group_rows(members, groups, sides, features)
    share = gradient_shares(members, groups, tile_lists, rows, weights, labels)
    step = math.sqrt(9 * channels * SIDE * SIDE / tile_lists.shape[1]) / math.sqrt(9 * channels)
    return new_shares(members, step, share, weights)


def solution(mesh):
    in_specs = (
        P("space", "clus", None),
        P("clus", None, None, None),
        P("clus", None),
        P("clus", None, None),
    )
    out_specs = P("clus", None, "space", None)
    members = 4
    return jax.shard_map(
        functools.partial(shards, members, mesh.shape["clus"]),
        mesh=mesh,
        in_specs=in_specs,
        out_specs=out_specs,
        check_vma=False,
    )
```

```python
import functools
import math

import jax
import jax.numpy as jnp
from jax import lax
from jax.experimental import pallas as pl
from jax.experimental.pallas import tpu as pltpu
from jax.sharding import PartitionSpec as P

SIDE = 8
BATCH = 4


def head_kernel(
    members, lists_ref, map_ref, weights_all, labels_all, grad_ref, wide, cols, acc, chosen, weights_ref, labels_ref, sems
):
    me = lax.axis_index("space")
    group, member = me // members, me % members
    clusters, length = labels_ref.shape[0], labels_ref.shape[1]
    mine = pl.ds(member * clusters, clusters)
    fetches = [
        pltpu.make_async_copy(weights_all.at[mine], weights_ref, sems.at[0]),
        pltpu.make_async_copy(labels_all.at[mine], labels_ref, sems.at[1]),
    ]
    for fetch in fetches:
        fetch.start()
    rows_all, columns, channels = map_ref.shape
    tiles = columns // SIDE
    bands = (rows_all - 2) // SIDE
    per_group = tiles * bands
    species = weights_ref.shape[2]
    scaling = 1.0 / math.sqrt(9 * channels)
    cells = SIDE * SIDE

    def widen(row, carry):
        wide[row, 1 : tiles + 1] = map_ref[row].astype(jnp.float32).reshape(tiles, SIDE, channels)
        wide[row, 0] = jnp.zeros((SIDE, channels), jnp.float32)
        wide[row, tiles + 1] = jnp.zeros((SIDE, channels), jnp.float32)
        return carry

    lax.fori_loop(0, rows_all, widen, 0)
    for fetch in fetches:
        fetch.wait()
    side_row = lax.broadcasted_iota(jnp.int32, (SIDE + 2, SIDE, channels), 1)

    def one_cluster(c, carry):
        def choose(k, count):
            chosen[count] = k
            return count + (lists_ref[member * clusters + c, k] // per_group == group).astype(jnp.int32)

        count = lax.fori_loop(0, length, choose, jnp.int32(0))
        acc[...] = jnp.zeros_like(acc)

        def one_batch(b, carry):
            targets = []
            for j in range(BATCH):
                slot = b * BATCH + j
                k = chosen[jnp.minimum(slot, count - 1)]
                tile = lists_ref[member * clusters + c, k] - group * per_group
                band, column = tile // tiles, tile % tiles
                rows = pl.ds(band * SIDE, SIDE + 2)
                left, mid, right = wide[rows, column], wide[rows, column + 1], wide[rows, column + 2]
                shifted = (
                    jnp.where(side_row == 0, pltpu.roll(left, 1, 1), pltpu.roll(mid, 1, 1)),
                    mid,
                    jnp.where(
                        side_row == SIDE - 1,
                        pltpu.roll(right, SIDE - 1, 1),
                        pltpu.roll(mid, SIDE - 1, 1),
                    ),
                )
                for dx in range(3):
                    flat = shifted[dx].reshape((SIDE + 2) * SIDE, channels)
                    for dy in range(3):
                        tap = 3 * dy + dx
                        cols[j * cells : (j + 1) * cells, tap * channels : (tap + 1) * channels] = flat[
                            dy * SIDE : dy * SIDE + cells
                        ].astype(jnp.bfloat16)
                targets.append(jnp.broadcast_to(labels_ref[c, pl.ds(k, 1), :].astype(jnp.float32), (cells, species)))
            target = jnp.concatenate(targets, axis=0)
            logits = jnp.dot(cols[...], weights_ref[c], preferred_element_type=jnp.float32)
            probability = jax.nn.sigmoid(logits * scaling)
            slots = b * BATCH + lax.broadcasted_iota(jnp.int32, (BATCH * cells, species), 0) // cells
            residual = jnp.where(slots < count, (probability - target) * (1.0 / cells), 0.0)
            residual = residual.astype(jnp.bfloat16)
            acc[...] += lax.dot_general(
                residual, cols[...], (((0,), (0,)), ((), ())), preferred_element_type=jnp.float32
            )
            return carry

        lax.fori_loop(0, (count + BATCH - 1) // BATCH, one_batch, 0)
        groups, depth = grad_ref.shape[0], grad_ref.shape[3]
        for tap in range(9):
            part = acc[:, tap * channels : (tap + 1) * channels].T.astype(grad_ref.dtype)
            grad_ref[:, c, tap] = part.reshape(groups, depth, species)
        return carry

    lax.fori_loop(0, clusters, one_cluster, 0)


def gradient_shares(members, groups, lists, rows, weights, labels):
    count, taps, channels, species = weights.shape
    rows_all, columns, _ = rows.shape
    clusters = count // members
    smem = pl.BlockSpec(memory_space=pltpu.SMEM)
    vmem = pl.BlockSpec(memory_space=pltpu.VMEM)
    whole = pl.BlockSpec(memory_space=pltpu.HBM)
    return pl.pallas_call(
        functools.partial(head_kernel, members),
        out_shape=jax.ShapeDtypeStruct(
            (groups, clusters, taps, channels // groups, species), jnp.bfloat16
        ),
        in_specs=[smem, vmem, whole, whole],
        out_specs=vmem,
        scratch_shapes=[
            pltpu.VMEM((rows_all, columns // SIDE + 2, SIDE, channels), jnp.float32),
            pltpu.VMEM((BATCH * SIDE * SIDE, taps * channels), jnp.bfloat16),
            pltpu.VMEM((species, taps * channels), jnp.float32),
            pltpu.SMEM((lists.shape[1],), jnp.int32),
            pltpu.VMEM((clusters, taps * channels, species), weights.dtype),
            pltpu.VMEM((clusters,) + labels.shape[1:], labels.dtype),
            pltpu.SemaphoreType.DMA((2,)),
        ],
        compiler_params=pltpu.CompilerParams(vmem_limit_bytes=40 * 2**20),
        cost_estimate=pl.CostEstimate(flops=5 * 10**9, bytes_accessed=6 * 10**6, transcendentals=0),
    )(lists, rows, weights.reshape(count, taps * channels, species), labels)


def remote(src, dst, send, recv, space, clus):
    return pltpu.make_async_remote_copy(
        src_ref=src,
        dst_ref=dst,
        send_sem=send,
        recv_sem=recv,
        device_id=(space, clus),
        device_id_type=pl.DeviceIdType.MESH,
    )


def greet(space, clus):
    barrier = pltpu.get_barrier_semaphore()
    pl.semaphore_signal(
        barrier, inc=1, device_id=(space, clus), device_id_type=pl.DeviceIdType.MESH
    )


def gather_kernel(
    members, groups, sides, own_ref, rows_ref, send, recv, edge_send, edge_recv, local
):
    me, side = lax.axis_index("space"), lax.axis_index("clus")
    group, member = me // members, me % members
    pair, core = member // 2, member % 2
    first = group * members
    sibling = first + pair * 2 + 1 - core
    width = own_ref.shape[1]
    last = rows_ref.shape[0] - 1
    half = SIDE // 2
    opposite = (1 - pair) * 2 + core
    across = [lax.rem(side + b, sides) for b in range(1, sides)]

    def spot(j, v, h):
        start = pl.multiple_of(v * width, width)
        return rows_ref.at[pl.ds(1 + j * SIDE + h * half, half), pl.ds(start, width)]

    def mark(j, v, h):
        return recv.at[(j * sides + v) * 2 + h]

    def edge(row, v):
        return rows_ref.at[pl.ds(row, 1), pl.ds(pl.multiple_of(v * width, width), width)]

    for v in across:
        greet(me, v)
    greet(first + opposite, side)
    greet(sibling, side)

    @pl.when(group > 0)
    def _():
        for v in range(sides):
            greet(first - 1, v)

    @pl.when(group < groups - 1)
    def _():
        for v in range(sides):
            greet(first + members, v)

    sends_up = (member == members - 1) & (group < groups - 1)
    sends_down = (member == 0) & (group > 0)
    barrier = pltpu.get_barrier_semaphore()
    edges = (sends_up | sends_down).astype(jnp.int32) * (members * sides)
    pl.semaphore_wait(barrier, sides + 1 + edges)

    def edge_copies(up):
        src = own_ref.at[pl.ds(SIDE - 1 if up else 0, 1)]
        start = first + members if up else first - members
        row, d = (0, 0) if up else (last, 1)
        return [
            remote(
                src,
                edge(row, side),
                edge_send.at[d * members * sides + j * sides + v],
                edge_recv.at[d * sides + side],
                start + j,
                v,
            )
            for j in range(members)
            for v in range(sides)
        ]

    @pl.when(sends_up)
    def _():
        for copy in edge_copies(True):
            copy.start()

    @pl.when(sends_down)
    def _():
        for copy in edge_copies(False):
            copy.start()

    sent = []

    def hand(src, j, v, h, space, clus):
        copy = remote(src, spot(j, v, h), send.at[len(sent)], mark(j, v, h), space, clus)
        copy.start()
        sent.append(copy)

    def arrived(j, v, h):
        here = spot(j, v, h)
        remote(here, here, send.at[0], mark(j, v, h), sibling, side).wait_recv()
        return here

    for h in range(2):
        own = own_ref.at[pl.ds(h * half, half)]
        other = own_ref.at[pl.ds((1 - h) * half, half)]
        for v in across:
            hand(own, member, side, h, me, v)
        hand(other, member, side, 1 - h, first + opposite, side)
    for h in range(2):
        hand(own_ref.at[pl.ds(h * half, half)], member, side, h, sibling, side)
    keep = [
        pltpu.make_async_copy(own_ref.at[pl.ds(h * half, half)], spot(member, side, h), local.at[h])
        for h in range(2)
    ]
    for copy in keep:
        copy.start()

    @pl.when(group == 0)
    def _():
        rows_ref[0] = jnp.zeros_like(rows_ref[0])

    @pl.when(group == groups - 1)
    def _():
        rows_ref[last] = jnp.zeros_like(rows_ref[last])

    for v in across:
        here = arrived(member, v, 0)
        hand(here, member, v, 0, first + opposite, side)
        hand(here, member, v, 0, sibling, side)
    here = arrived(opposite, side, 1)
    for v in across:
        hand(here, opposite, side, 1, me, v)
    hand(here, opposite, side, 1, sibling, side)
    for v in across:
        hand(arrived(member, v, 1), member, v, 1, sibling, side)
    hand(arrived(opposite, side, 0), opposite, side, 0, sibling, side)
    for v in across:
        for h in range(2):
            hand(arrived(opposite, v, h), opposite, v, h, sibling, side)
    for p in range(2):
        for v in range(sides):
            for h in range(2):
                arrived(p * 2 + 1 - core, v, h)

    @pl.when(group > 0)
    def _():
        for v in range(sides):
            remote(edge(0, v), edge(0, v), edge_send.at[0], edge_recv.at[v], sibling, side).wait_recv()

    @pl.when(group < groups - 1)
    def _():
        for v in range(sides):
            mark = edge_recv.at[sides + v]
            remote(edge(last, v), edge(last, v), edge_send.at[0], mark, sibling, side).wait_recv()

    for copy in keep:
        copy.wait()
    for copy in sent:
        copy.wait_send()

    @pl.when(sends_up)
    def _():
        for copy in edge_copies(True):
            copy.wait_send()

    @pl.when(sends_down)
    def _():
        for copy in edge_copies(False):
            copy.wait_send()


def group_rows(members, groups, sides, features):
    side_rows, width, channels = features.shape
    count = members * sides
    dma = pltpu.SemaphoreType.DMA
    return pl.pallas_call(
        functools.partial(gather_kernel, members, groups, sides),
        out_shape=jax.ShapeDtypeStruct(
            (members * side_rows + 2, sides * width, channels), features.dtype
        ),
        in_specs=[pl.BlockSpec(memory_space=pltpu.HBM)],
        out_specs=pl.BlockSpec(memory_space=pltpu.VMEM),
        scratch_shapes=[
            dma((4 * count,)),
            dma((2 * count,)),
            dma((2 * count,)),
            dma((2 * sides,)),
            dma((2,)),
        ],
        compiler_params=pltpu.CompilerParams(
            collective_id=0, has_side_effects=True, vmem_limit_bytes=16 * 2**20
        ),
        cost_estimate=pl.CostEstimate(flops=0, bytes_accessed=4 * 10**6, transcendentals=0),
    )(features)


def reduce_kernel(
    members,
    groups,
    step,
    share_ref,
    weights_ref,
    new_ref,
    old,
    near,
    relay,
    joined,
    far,
    fresh,
    near_send,
    near_recv,
    relay_send,
    relay_recv,
    far_send,
    far_recv,
    out_send,
    out_recv,
    local,
):
    me, side = lax.axis_index("space"), lax.axis_index("clus")
    group, member = me // members, me % members
    clusters, taps, depth, species = old.shape
    piece = depth // members
    pairs = groups // 2
    pair = group // 2

    def joint_of(p):
        return p * 2 + (p < pairs // 2).astype(jnp.int32)

    def at(g):
        return g * members + member

    partner = pair * 2 + 1 - group % 2
    is_joint = group == joint_of(pair)
    not_joint = group != joint_of(pair)

    kept_weights = pltpu.make_async_copy(
        weights_ref.at[
            pl.ds(member * clusters, clusters),
            :,
            pl.ds(pl.multiple_of(group * depth, depth), depth),
        ],
        old,
        local.at[clusters],
    )
    kept_weights.start()

    greet(at(partner), side)
    for q in range(1, pairs):
        greet(at(joint_of(lax.rem(pair + q, pairs))), side)
    for o in range(1, members):
        greet(group * members + lax.rem(member + o, members), side)
    pl.semaphore_wait(
        pltpu.get_barrier_semaphore(), members + is_joint.astype(jnp.int32) * (2 * (pairs - 1))
    )

    parts = [(c, q, e) for c in range(clusters) for q in range(1, pairs) for e in range(2)]

    def index(c, q, e):
        return (c * (pairs - 1) + q - 1) * 2 + e

    def to_partner(c):
        return remote(
            share_ref.at[partner, c], near.at[c], near_send.at[c], near_recv.at[c], at(partner), side
        )

    def to_joint(c, q, e):
        i = index(c, q, e)
        return remote(
            share_ref.at[lax.rem(pair + q, pairs) * 2 + e, c],
            relay.at[i],
            relay_send.at[i],
            relay_recv.at[i],
            at(partner),
            side,
        )

    def across(c, q, e):
        i = index(c, q, e)
        j = c * (pairs - 1) + q - 1
        to = lax.rem(pair + q, pairs) * 2 + e
        return remote(joined.at[i], far.at[j], far_send.at[i], far_recv.at[j], at(to), side)

    def handed(c, o):
        to = lax.rem(member + o, members)
        i = c * members + o
        return remote(
            fresh.at[to, c],
            new_ref.at[member * clusters + c],
            out_send.at[i],
            out_recv.at[i],
            group * members + to,
            side,
        )

    def kept(c):
        return pltpu.make_async_copy(
            fresh.at[member, c], new_ref.at[member * clusters + c], local.at[c]
        )

    @pl.when(not_joint)
    def _():
        for c, q, e in parts:
            to_joint(c, q, e).start()

    for c in range(clusters):
        to_partner(c).start()

    @pl.when(is_joint)
    def _():
        for c, q, e in parts:
            to_joint(c, q, e).wait_recv()
            i, to = index(c, q, e), lax.rem(pair + q, pairs) * 2 + e

            def join(tap, carry, i=i, to=to, c=c):
                total = share_ref[to, c, tap].astype(jnp.float32) + relay[i, tap].astype(jnp.float32)
                joined[i, tap] = total.astype(joined.dtype)
                return carry

            lax.fori_loop(0, taps, join, 0)
            across(c, q, e).start()

    kept_weights.wait()
    for c in range(clusters):
        to_partner(c).wait_recv()
        for q in range(1, pairs):
            across(c, q, 0).wait_recv()

        def one_tap(tap, carry, c=c):
            total = share_ref[group, c, tap].astype(jnp.float32) + near[c, tap].astype(jnp.float32)
            for q in range(1, pairs):
                total = total + far[c * (pairs - 1) + q - 1, tap].astype(jnp.float32)
            new = old[c, tap].astype(jnp.float32) - step * total
            fresh[:, c, tap] = new.reshape(members, piece, species).astype(fresh.dtype)
            return carry

        lax.fori_loop(0, taps, one_tap, 0)
        for o in range(1, members):
            handed(c, o).start()
        kept(c).start()
    for c in range(clusters):
        kept(c).wait()
        for o in range(1, members):
            handed(c, o).wait()
        to_partner(c).wait_send()

    @pl.when(not_joint)
    def _():
        for c, q, e in parts:
            to_joint(c, q, e).wait_send()

    @pl.when(is_joint)
    def _():
        for c, q, e in parts:
            across(c, q, e).wait_send()


def new_shares(members, step, share, weights):
    groups, clusters, taps, depth, species = share.shape
    away = clusters * (groups // 2 - 1)
    block = (taps, depth, species)
    dma = pltpu.SemaphoreType.DMA
    vmem = pl.BlockSpec(memory_space=pltpu.VMEM)
    return pl.pallas_call(
        functools.partial(reduce_kernel, members, groups, step),
        out_shape=jax.ShapeDtypeStruct(
            (members * clusters, taps, depth // members, species), weights.dtype
        ),
        in_specs=[vmem, pl.BlockSpec(memory_space=pltpu.HBM)],
        out_specs=vmem,
        scratch_shapes=[
            pltpu.VMEM((clusters,) + block, weights.dtype),
            pltpu.VMEM((clusters,) + block, share.dtype),
            pltpu.VMEM((2 * away,) + block, share.dtype),
            pltpu.VMEM((2 * away,) + block, share.dtype),
            pltpu.VMEM((away,) + block, share.dtype),
            pltpu.VMEM((members, clusters, taps, depth // members, species), weights.dtype),
            dma((clusters,)),
            dma((clusters,)),
            dma((2 * away,)),
            dma((2 * away,)),
            dma((2 * away,)),
            dma((away,)),
            dma((clusters * members,)),
            dma((clusters * members,)),
            dma((clusters + 1,)),
        ],
        compiler_params=pltpu.CompilerParams(
            collective_id=1, has_side_effects=True, vmem_limit_bytes=24 * 2**20
        ),
        cost_estimate=pl.CostEstimate(flops=10**6, bytes_accessed=4 * 10**6, transcendentals=0),
    )(share, weights)


def shards(members, sides, features, weights, tile_lists, labels):
    groups = lax.axis_size("space") // members
    channels = weights.shape[2]
    rows = group_rows(members, groups, sides, features)
    share = gradient_shares(members, groups, tile_lists, rows, weights, labels)
    step = math.sqrt(9 * channels * SIDE * SIDE / tile_lists.shape[1]) / math.sqrt(9 * channels)
    return new_shares(members, step, share, weights)


def solution(mesh):
    in_specs = (
        P("space", "clus", None),
        P("clus", None, None, None),
        P("clus", None),
        P("clus", None, None),
    )
    out_specs = P("clus", None, "space", None)
    members = 4
    return jax.shard_map(
        functools.partial(shards, members, mesh.shape["clus"]),
        mesh=mesh,
        in_specs=in_specs,
        out_specs=out_specs,
        check_vma=False,
    )
```

```python
import functools
import math

import jax
import jax.numpy as jnp
from jax import lax
from jax.experimental import pallas as pl
from jax.experimental.pallas import tpu as pltpu
from jax.sharding import PartitionSpec as P

SIDE = 8
BATCH = 4


def head_kernel(
    members, lists_ref, map_ref, weights_all, labels_all, grad_ref, wide, cols, acc, chosen, weights_ref, labels_ref, sems
):
    me = lax.axis_index("space")
    group, member = me // members, me % members
    clusters, length = labels_ref.shape[0], labels_ref.shape[1]
    mine = pl.ds(member * clusters, clusters)
    fetches = [
        pltpu.make_async_copy(weights_all.at[mine], weights_ref, sems.at[0]),
        pltpu.make_async_copy(labels_all.at[mine], labels_ref, sems.at[1]),
    ]
    for fetch in fetches:
        fetch.start()
    rows_all, columns, channels = map_ref.shape
    tiles = columns // SIDE
    bands = (rows_all - 2) // SIDE
    per_group = tiles * bands
    species = weights_ref.shape[2]
    scaling = 1.0 / math.sqrt(9 * channels)
    cells = SIDE * SIDE

    def widen(row, carry):
        wide[row, 1 : tiles + 1] = map_ref[row].astype(jnp.float32).reshape(tiles, SIDE, channels)
        wide[row, 0] = jnp.zeros((SIDE, channels), jnp.float32)
        wide[row, tiles + 1] = jnp.zeros((SIDE, channels), jnp.float32)
        return carry

    lax.fori_loop(0, rows_all, widen, 0)
    for fetch in fetches:
        fetch.wait()
    side_row = lax.broadcasted_iota(jnp.int32, (SIDE + 2, SIDE, channels), 1)

    def one_cluster(c, carry):
        def choose(k, count):
            chosen[count] = k
            return count + (lists_ref[member * clusters + c, k] // per_group == group).astype(jnp.int32)

        count = lax.fori_loop(0, length, choose, jnp.int32(0))
        acc[...] = jnp.zeros_like(acc)

        def one_batch(b, carry):
            targets = []
            for j in range(BATCH):
                slot = b * BATCH + j
                k = chosen[jnp.minimum(slot, count - 1)]
                tile = lists_ref[member * clusters + c, k] - group * per_group
                band, column = tile // tiles, tile % tiles
                rows = pl.ds(band * SIDE, SIDE + 2)
                left, mid, right = wide[rows, column], wide[rows, column + 1], wide[rows, column + 2]
                shifted = (
                    jnp.where(side_row == 0, pltpu.roll(left, 1, 1), pltpu.roll(mid, 1, 1)),
                    mid,
                    jnp.where(
                        side_row == SIDE - 1,
                        pltpu.roll(right, SIDE - 1, 1),
                        pltpu.roll(mid, SIDE - 1, 1),
                    ),
                )
                for dx in range(3):
                    flat = shifted[dx].reshape((SIDE + 2) * SIDE, channels)
                    for dy in range(3):
                        tap = 3 * dy + dx
                        cols[j * cells : (j + 1) * cells, tap * channels : (tap + 1) * channels] = flat[
                            dy * SIDE : dy * SIDE + cells
                        ].astype(jnp.bfloat16)
                targets.append(jnp.broadcast_to(labels_ref[c, pl.ds(k, 1), :].astype(jnp.float32), (cells, species)))
            target = jnp.concatenate(targets, axis=0)
            logits = jnp.dot(cols[...], weights_ref[c], preferred_element_type=jnp.float32)
            probability = jax.nn.sigmoid(logits * scaling)
            slots = b * BATCH + lax.broadcasted_iota(jnp.int32, (BATCH * cells, species), 0) // cells
            residual = jnp.where(slots < count, (probability - target) * (1.0 / cells), 0.0)
            residual = residual.astype(jnp.bfloat16)
            acc[...] += lax.dot_general(
                residual, cols[...], (((0,), (0,)), ((), ())), preferred_element_type=jnp.float32
            )
            return carry

        lax.fori_loop(0, (count + BATCH - 1) // BATCH, one_batch, 0)
        groups, depth = grad_ref.shape[0], grad_ref.shape[3]
        for tap in range(9):
            part = acc[:, tap * channels : (tap + 1) * channels].T.astype(grad_ref.dtype)
            grad_ref[:, c, tap] = part.reshape(groups, depth, species)
        return carry

    lax.fori_loop(0, clusters, one_cluster, 0)


def gradient_shares(members, groups, lists, rows, weights, labels):
    count, taps, channels, species = weights.shape
    rows_all, columns, _ = rows.shape
    clusters = count // members
    smem = pl.BlockSpec(memory_space=pltpu.SMEM)
    vmem = pl.BlockSpec(memory_space=pltpu.VMEM)
    whole = pl.BlockSpec(memory_space=pltpu.HBM)
    return pl.pallas_call(
        functools.partial(head_kernel, members),
        out_shape=jax.ShapeDtypeStruct(
            (groups, clusters, taps, channels // groups, species), jnp.bfloat16
        ),
        in_specs=[smem, vmem, whole, whole],
        out_specs=vmem,
        scratch_shapes=[
            pltpu.VMEM((rows_all, columns // SIDE + 2, SIDE, channels), jnp.float32),
            pltpu.VMEM((BATCH * SIDE * SIDE, taps * channels), jnp.bfloat16),
            pltpu.VMEM((species, taps * channels), jnp.float32),
            pltpu.SMEM((lists.shape[1],), jnp.int32),
            pltpu.VMEM((clusters, taps * channels, species), weights.dtype),
            pltpu.VMEM((clusters,) + labels.shape[1:], labels.dtype),
            pltpu.SemaphoreType.DMA((2,)),
        ],
        compiler_params=pltpu.CompilerParams(vmem_limit_bytes=57 * 2**20),
        cost_estimate=pl.CostEstimate(flops=5 * 10**9, bytes_accessed=6 * 10**6, transcendentals=0),
    )(lists, rows, weights.reshape(count, taps * channels, species), labels)


def remote(src, dst, send, recv, space, clus):
    return pltpu.make_async_remote_copy(
        src_ref=src,
        dst_ref=dst,
        send_sem=send,
        recv_sem=recv,
        device_id=(space, clus),
        device_id_type=pl.DeviceIdType.MESH,
    )


def greet(space, clus):
    barrier = pltpu.get_barrier_semaphore()
    pl.semaphore_signal(
        barrier, inc=1, device_id=(space, clus), device_id_type=pl.DeviceIdType.MESH
    )


def gather_kernel(
    members, groups, sides, own_ref, rows_ref, send, recv, edge_send, edge_recv, local
):
    me, side = lax.axis_index("space"), lax.axis_index("clus")
    group, member = me // members, me % members
    pair, core = member // 2, member % 2
    first = group * members
    sibling = first + pair * 2 + 1 - core
    width = own_ref.shape[1]
    last = rows_ref.shape[0] - 1
    half = SIDE // 2
    opposite = (1 - pair) * 2 + core
    across = [lax.rem(side + b, sides) for b in range(1, sides)]

    def spot(j, v, h):
        start = pl.multiple_of(v * width, width)
        return rows_ref.at[pl.ds(1 + j * SIDE + h * half, half), pl.ds(start, width)]

    def mark(j, v, h):
        return recv.at[(j * sides + v) * 2 + h]

    def edge(row, v):
        return rows_ref.at[pl.ds(row, 1), pl.ds(pl.multiple_of(v * width, width), width)]

    for v in across:
        greet(me, v)
    greet(first + opposite, side)
    greet(sibling, side)

    @pl.when(group > 0)
    def _():
        for v in range(sides):
            greet(first - 1, v)

    @pl.when(group < groups - 1)
    def _():
        for v in range(sides):
            greet(first + members, v)

    sends_up = (member == members - 1) & (group < groups - 1)
    sends_down = (member == 0) & (group > 0)
    barrier = pltpu.get_barrier_semaphore()
    edges = (sends_up | sends_down).astype(jnp.int32) * (members * sides)
    pl.semaphore_wait(barrier, sides + 1 + edges)

    def edge_copies(up):
        src = own_ref.at[pl.ds(SIDE - 1 if up else 0, 1)]
        start = first + members if up else first - members
        row, d = (0, 0) if up else (last, 1)
        return [
            remote(
                src,
                edge(row, side),
                edge_send.at[d * members * sides + j * sides + v],
                edge_recv.at[d * sides + side],
                start + j,
                v,
            )
            for j in range(members)
            for v in range(sides)
        ]

    @pl.when(sends_up)
    def _():
        for copy in edge_copies(True):
            copy.start()

    @pl.when(sends_down)
    def _():
        for copy in edge_copies(False):
            copy.start()

    sent = []

    def hand(src, j, v, h, space, clus):
        copy = remote(src, spot(j, v, h), send.at[len(sent)], mark(j, v, h), space, clus)
        copy.start()
        sent.append(copy)

    def arrived(j, v, h):
        here = spot(j, v, h)
        remote(here, here, send.at[0], mark(j, v, h), sibling, side).wait_recv()
        return here

    for h in range(2):
        own = own_ref.at[pl.ds(h * half, half)]
        other = own_ref.at[pl.ds((1 - h) * half, half)]
        for v in across:
            hand(own, member, side, h, me, v)
        hand(other, member, side, 1 - h, first + opposite, side)
    for h in range(2):
        hand(own_ref.at[pl.ds(h * half, half)], member, side, h, sibling, side)
    keep = [
        pltpu.make_async_copy(own_ref.at[pl.ds(h * half, half)], spot(member, side, h), local.at[h])
        for h in range(2)
    ]
    for copy in keep:
        copy.start()

    @pl.when(group == 0)
    def _():
        rows_ref[0] = jnp.zeros_like(rows_ref[0])

    @pl.when(group == groups - 1)
    def _():
        rows_ref[last] = jnp.zeros_like(rows_ref[last])

    for v in across:
        here = arrived(member, v, 0)
        hand(here, member, v, 0, first + opposite, side)
        hand(here, member, v, 0, sibling, side)
    here = arrived(opposite, side, 1)
    for v in across:
        hand(here, opposite, side, 1, me, v)
    hand(here, opposite, side, 1, sibling, side)
    for v in across:
        hand(arrived(member, v, 1), member, v, 1, sibling, side)
    hand(arrived(opposite, side, 0), opposite, side, 0, sibling, side)
    for v in across:
        for h in range(2):
            hand(arrived(opposite, v, h), opposite, v, h, sibling, side)
    for p in range(2):
        for v in range(sides):
            for h in range(2):
                arrived(p * 2 + 1 - core, v, h)

    @pl.when(group > 0)
    def _():
        for v in range(sides):
            remote(edge(0, v), edge(0, v), edge_send.at[0], edge_recv.at[v], sibling, side).wait_recv()

    @pl.when(group < groups - 1)
    def _():
        for v in range(sides):
            mark = edge_recv.at[sides + v]
            remote(edge(last, v), edge(last, v), edge_send.at[0], mark, sibling, side).wait_recv()

    for copy in keep:
        copy.wait()
    for copy in sent:
        copy.wait_send()

    @pl.when(sends_up)
    def _():
        for copy in edge_copies(True):
            copy.wait_send()

    @pl.when(sends_down)
    def _():
        for copy in edge_copies(False):
            copy.wait_send()


def group_rows(members, groups, sides, features):
    side_rows, width, channels = features.shape
    count = members * sides
    dma = pltpu.SemaphoreType.DMA
    return pl.pallas_call(
        functools.partial(gather_kernel, members, groups, sides),
        out_shape=jax.ShapeDtypeStruct(
            (members * side_rows + 2, sides * width, channels), features.dtype
        ),
        in_specs=[pl.BlockSpec(memory_space=pltpu.HBM)],
        out_specs=pl.BlockSpec(memory_space=pltpu.VMEM),
        scratch_shapes=[
            dma((4 * count,)),
            dma((2 * count,)),
            dma((2 * count,)),
            dma((2 * sides,)),
            dma((2,)),
        ],
        compiler_params=pltpu.CompilerParams(
            collective_id=0, has_side_effects=True, vmem_limit_bytes=16 * 2**20
        ),
        cost_estimate=pl.CostEstimate(flops=0, bytes_accessed=4 * 10**6, transcendentals=0),
    )(features)


def reduce_kernel(
    members,
    groups,
    step,
    share_ref,
    weights_ref,
    new_ref,
    old,
    near,
    relay,
    joined,
    far,
    fresh,
    near_send,
    near_recv,
    relay_send,
    relay_recv,
    far_send,
    far_recv,
    out_send,
    out_recv,
    local,
):
    me, side = lax.axis_index("space"), lax.axis_index("clus")
    group, member = me // members, me % members
    clusters, taps, depth, species = old.shape
    piece = depth // members
    pairs = groups // 2
    pair = group // 2

    def joint_of(p):
        return p * 2 + (p < pairs // 2).astype(jnp.int32)

    def at(g):
        return g * members + member

    partner = pair * 2 + 1 - group % 2
    is_joint = group == joint_of(pair)
    not_joint = group != joint_of(pair)

    kept_weights = pltpu.make_async_copy(
        weights_ref.at[
            pl.ds(member * clusters, clusters),
            :,
            pl.ds(pl.multiple_of(group * depth, depth), depth),
        ],
        old,
        local.at[clusters],
    )
    kept_weights.start()

    greet(at(partner), side)
    for q in range(1, pairs):
        greet(at(joint_of(lax.rem(pair + q, pairs))), side)
    for o in range(1, members):
        greet(group * members + lax.rem(member + o, members), side)
    pl.semaphore_wait(
        pltpu.get_barrier_semaphore(), members + is_joint.astype(jnp.int32) * (2 * (pairs - 1))
    )

    parts = [(c, q, e) for c in range(clusters) for q in range(1, pairs) for e in range(2)]

    def index(c, q, e):
        return (c * (pairs - 1) + q - 1) * 2 + e

    def to_partner(c):
        return remote(
            share_ref.at[partner, c], near.at[c], near_send.at[c], near_recv.at[c], at(partner), side
        )

    def to_joint(c, q, e):
        i = index(c, q, e)
        return remote(
            share_ref.at[lax.rem(pair + q, pairs) * 2 + e, c],
            relay.at[i],
            relay_send.at[i],
            relay_recv.at[i],
            at(partner),
            side,
        )

    def across(c, q, e):
        i = index(c, q, e)
        j = c * (pairs - 1) + q - 1
        to = lax.rem(pair + q, pairs) * 2 + e
        return remote(joined.at[i], far.at[j], far_send.at[i], far_recv.at[j], at(to), side)

    def handed(c, o):
        to = lax.rem(member + o, members)
        i = c * members + o
        return remote(
            fresh.at[to, c],
            new_ref.at[member * clusters + c],
            out_send.at[i],
            out_recv.at[i],
            group * members + to,
            side,
        )

    def kept(c):
        return pltpu.make_async_copy(
            fresh.at[member, c], new_ref.at[member * clusters + c], local.at[c]
        )

    @pl.when(not_joint)
    def _():
        for c, q, e in parts:
            to_joint(c, q, e).start()

    for c in range(clusters):
        to_partner(c).start()

    @pl.when(is_joint)
    def _():
        for c, q, e in parts:
            to_joint(c, q, e).wait_recv()
            i, to = index(c, q, e), lax.rem(pair + q, pairs) * 2 + e

            def join(tap, carry, i=i, to=to, c=c):
                total = share_ref[to, c, tap].astype(jnp.float32) + relay[i, tap].astype(jnp.float32)
                joined[i, tap] = total.astype(joined.dtype)
                return carry

            lax.fori_loop(0, taps, join, 0)
            across(c, q, e).start()

    kept_weights.wait()
    for c in range(clusters):
        to_partner(c).wait_recv()
        for q in range(1, pairs):
            across(c, q, 0).wait_recv()

        def one_tap(tap, carry, c=c):
            total = share_ref[group, c, tap].astype(jnp.float32) + near[c, tap].astype(jnp.float32)
            for q in range(1, pairs):
                total = total + far[c * (pairs - 1) + q - 1, tap].astype(jnp.float32)
            new = old[c, tap].astype(jnp.float32) - step * total
            fresh[:, c, tap] = new.reshape(members, piece, species).astype(fresh.dtype)
            return carry

        lax.fori_loop(0, taps, one_tap, 0)
        for o in range(1, members):
            handed(c, o).start()
        kept(c).start()
    for c in range(clusters):
        kept(c).wait()
        for o in range(1, members):
            handed(c, o).wait()
        to_partner(c).wait_send()

    @pl.when(not_joint)
    def _():
        for c, q, e in parts:
            to_joint(c, q, e).wait_send()

    @pl.when(is_joint)
    def _():
        for c, q, e in parts:
            across(c, q, e).wait_send()


def new_shares(members, step, share, weights):
    groups, clusters, taps, depth, species = share.shape
    away = clusters * (groups // 2 - 1)
    block = (taps, depth, species)
    dma = pltpu.SemaphoreType.DMA
    vmem = pl.BlockSpec(memory_space=pltpu.VMEM)
    return pl.pallas_call(
        functools.partial(reduce_kernel, members, groups, step),
        out_shape=jax.ShapeDtypeStruct(
            (members * clusters, taps, depth // members, species), weights.dtype
        ),
        in_specs=[vmem, pl.BlockSpec(memory_space=pltpu.HBM)],
        out_specs=vmem,
        scratch_shapes=[
            pltpu.VMEM((clusters,) + block, weights.dtype),
            pltpu.VMEM((clusters,) + block, share.dtype),
            pltpu.VMEM((2 * away,) + block, share.dtype),
            pltpu.VMEM((2 * away,) + block, share.dtype),
            pltpu.VMEM((away,) + block, share.dtype),
            pltpu.VMEM((members, clusters, taps, depth // members, species), weights.dtype),
            dma((clusters,)),
            dma((clusters,)),
            dma((2 * away,)),
            dma((2 * away,)),
            dma((2 * away,)),
            dma((away,)),
            dma((clusters * members,)),
            dma((clusters * members,)),
            dma((clusters + 1,)),
        ],
        compiler_params=pltpu.CompilerParams(
            collective_id=1, has_side_effects=True, vmem_limit_bytes=57 * 2**20
        ),
        cost_estimate=pl.CostEstimate(flops=10**6, bytes_accessed=4 * 10**6, transcendentals=0),
    )(share, weights)


def shards(members, sides, features, weights, tile_lists, labels):
    groups = lax.axis_size("space") // members
    channels = weights.shape[2]
    rows = group_rows(members, groups, sides, features)
    share = gradient_shares(members, groups, tile_lists, rows, weights, labels)
    step = math.sqrt(9 * channels * SIDE * SIDE / tile_lists.shape[1]) / math.sqrt(9 * channels)
    return new_shares(members, step, share, weights)


def solution(mesh):
    in_specs = (
        P("space", "clus", None),
        P("clus", None, None, None),
        P("clus", None),
        P("clus", None, None),
    )
    out_specs = P("clus", None, "space", None)
    members = 4
    return jax.shard_map(
        functools.partial(shards, members, mesh.shape["clus"]),
        mesh=mesh,
        in_specs=in_specs,
        out_specs=out_specs,
        check_vma=False,
    )
```

```python
import functools
import math

import jax
import jax.numpy as jnp
from jax import lax
from jax.experimental import pallas as pl
from jax.experimental.pallas import tpu as pltpu
from jax.sharding import PartitionSpec as P

SIDE = 8
BATCH = 4


def head_kernel(
    members, lists_ref, map_ref, weights_all, labels_all, grad_ref, wide, cols, acc, chosen, weights_ref, labels_ref, sems
):
    me = lax.axis_index("space")
    group, member = me // members, me % members
    clusters, length = labels_ref.shape[0], labels_ref.shape[1]
    mine = pl.ds(member * clusters, clusters)
    fetches = [
        pltpu.make_async_copy(weights_all.at[mine], weights_ref, sems.at[0]),
        pltpu.make_async_copy(labels_all.at[mine], labels_ref, sems.at[1]),
    ]
    for fetch in fetches:
        fetch.start()
    rows_all, columns, channels = map_ref.shape
    tiles = columns // SIDE
    bands = (rows_all - 2) // SIDE
    per_group = tiles * bands
    species = weights_ref.shape[2]
    scaling = 1.0 / math.sqrt(9 * channels)
    cells = SIDE * SIDE

    def widen(row, carry):
        wide[row, 1 : tiles + 1] = map_ref[row].astype(jnp.float32).reshape(tiles, SIDE, channels)
        wide[row, 0] = jnp.zeros((SIDE, channels), jnp.float32)
        wide[row, tiles + 1] = jnp.zeros((SIDE, channels), jnp.float32)
        return carry

    lax.fori_loop(0, rows_all, widen, 0)
    for fetch in fetches:
        fetch.wait()
    side_row = lax.broadcasted_iota(jnp.int32, (SIDE + 2, SIDE, channels), 1)

    def one_cluster(c, carry):
        def choose(k, count):
            chosen[count] = k
            return count + (lists_ref[member * clusters + c, k] // per_group == group).astype(jnp.int32)

        count = lax.fori_loop(0, length, choose, jnp.int32(0))
        acc[...] = jnp.zeros_like(acc)

        def one_batch(b, carry):
            targets = []
            for j in range(BATCH):
                slot = b * BATCH + j
                k = chosen[jnp.minimum(slot, count - 1)]
                tile = lists_ref[member * clusters + c, k] - group * per_group
                band, column = tile // tiles, tile % tiles
                rows = pl.ds(band * SIDE, SIDE + 2)
                left, mid, right = wide[rows, column], wide[rows, column + 1], wide[rows, column + 2]
                shifted = (
                    jnp.where(side_row == 0, pltpu.roll(left, 1, 1), pltpu.roll(mid, 1, 1)),
                    mid,
                    jnp.where(
                        side_row == SIDE - 1,
                        pltpu.roll(right, SIDE - 1, 1),
                        pltpu.roll(mid, SIDE - 1, 1),
                    ),
                )
                for dx in range(3):
                    flat = shifted[dx].reshape((SIDE + 2) * SIDE, channels)
                    for dy in range(3):
                        tap = 3 * dy + dx
                        cols[j * cells : (j + 1) * cells, tap * channels : (tap + 1) * channels] = flat[
                            dy * SIDE : dy * SIDE + cells
                        ].astype(jnp.bfloat16)
                targets.append(jnp.broadcast_to(labels_ref[c, pl.ds(k, 1), :].astype(jnp.float32), (cells, species)))
            target = jnp.concatenate(targets, axis=0)
            logits = jnp.dot(cols[...], weights_ref[c], preferred_element_type=jnp.float32)
            probability = jax.nn.sigmoid(logits * scaling)
            slots = b * BATCH + lax.broadcasted_iota(jnp.int32, (BATCH * cells, species), 0) // cells
            residual = jnp.where(slots < count, (probability - target) * (1.0 / cells), 0.0)
            residual = residual.astype(jnp.bfloat16)
            acc[...] += lax.dot_general(
                residual, cols[...], (((0,), (0,)), ((), ())), preferred_element_type=jnp.float32
            )
            return carry

        lax.fori_loop(0, (count + BATCH - 1) // BATCH, one_batch, 0)
        groups, depth = grad_ref.shape[0], grad_ref.shape[3]
        for tap in range(9):
            part = acc[:, tap * channels : (tap + 1) * channels].T.astype(grad_ref.dtype)
            grad_ref[:, c, tap] = part.reshape(groups, depth, species)
        return carry

    lax.fori_loop(0, clusters, one_cluster, 0)


def gradient_shares(members, groups, lists, rows, weights, labels):
    count, taps, channels, species = weights.shape
    rows_all, columns, _ = rows.shape
    clusters = count // members
    smem = pl.BlockSpec(memory_space=pltpu.SMEM)
    vmem = pl.BlockSpec(memory_space=pltpu.VMEM)
    whole = pl.BlockSpec(memory_space=pltpu.HBM)
    return pl.pallas_call(
        functools.partial(head_kernel, members),
        out_shape=jax.ShapeDtypeStruct(
            (groups, clusters, taps, channels // groups, species), jnp.bfloat16
        ),
        in_specs=[smem, vmem, whole, whole],
        out_specs=vmem,
        scratch_shapes=[
            pltpu.VMEM((rows_all, columns // SIDE + 2, SIDE, channels), jnp.float32),
            pltpu.VMEM((BATCH * SIDE * SIDE, taps * channels), jnp.bfloat16),
            pltpu.VMEM((species, taps * channels), jnp.float32),
            pltpu.SMEM((lists.shape[1],), jnp.int32),
            pltpu.VMEM((clusters, taps * channels, species), weights.dtype),
            pltpu.VMEM((clusters,) + labels.shape[1:], labels.dtype),
            pltpu.SemaphoreType.DMA((2,)),
        ],
        compiler_params=pltpu.CompilerParams(vmem_limit_bytes=40 * 2**20),
        cost_estimate=pl.CostEstimate(flops=5 * 10**9, bytes_accessed=6 * 10**6, transcendentals=0),
    )(lists, rows, weights.reshape(count, taps * channels, species), labels)


def remote(src, dst, send, recv, space, clus):
    return pltpu.make_async_remote_copy(
        src_ref=src,
        dst_ref=dst,
        send_sem=send,
        recv_sem=recv,
        device_id=(space, clus),
        device_id_type=pl.DeviceIdType.MESH,
    )


def greet(space, clus):
    barrier = pltpu.get_barrier_semaphore()
    pl.semaphore_signal(
        barrier, inc=1, device_id=(space, clus), device_id_type=pl.DeviceIdType.MESH
    )


def gather_kernel(
    members, groups, sides, own_ref, rows_ref, send, recv, edge_send, edge_recv, local
):
    me, side = lax.axis_index("space"), lax.axis_index("clus")
    group, member = me // members, me % members
    pair, core = member // 2, member % 2
    first = group * members
    sibling = first + pair * 2 + 1 - core
    width = own_ref.shape[1]
    last = rows_ref.shape[0] - 1
    half = SIDE // 2
    opposite = (1 - pair) * 2 + core
    across = [lax.rem(side + b, sides) for b in range(1, sides)]

    def spot(j, v, h):
        start = pl.multiple_of(v * width, width)
        return rows_ref.at[pl.ds(1 + j * SIDE + h * half, half), pl.ds(start, width)]

    def mark(j, v, h):
        return recv.at[(j * sides + v) * 2 + h]

    def edge(row, v):
        return rows_ref.at[pl.ds(row, 1), pl.ds(pl.multiple_of(v * width, width), width)]

    for v in across:
        greet(me, v)
    greet(first + opposite, side)
    greet(sibling, side)

    @pl.when(group > 0)
    def _():
        for v in range(sides):
            greet(first - 1, v)

    @pl.when(group < groups - 1)
    def _():
        for v in range(sides):
            greet(first + members, v)

    sends_up = (member == members - 1) & (group < groups - 1)
    sends_down = (member == 0) & (group > 0)
    barrier = pltpu.get_barrier_semaphore()
    edges = (sends_up | sends_down).astype(jnp.int32) * (members * sides)
    pl.semaphore_wait(barrier, sides + 1 + edges)

    def edge_copies(up):
        src = own_ref.at[pl.ds(SIDE - 1 if up else 0, 1)]
        start = first + members if up else first - members
        row, d = (0, 0) if up else (last, 1)
        return [
            remote(
                src,
                edge(row, side),
                edge_send.at[d * members * sides + j * sides + v],
                edge_recv.at[d * sides + side],
                start + j,
                v,
            )
            for j in range(members)
            for v in range(sides)
        ]

    @pl.when(sends_up)
    def _():
        for copy in edge_copies(True):
            copy.start()

    @pl.when(sends_down)
    def _():
        for copy in edge_copies(False):
            copy.start()

    sent = []

    def hand(src, j, v, h, space, clus):
        copy = remote(src, spot(j, v, h), send.at[len(sent)], mark(j, v, h), space, clus)
        copy.start()
        sent.append(copy)

    def arrived(j, v, h):
        here = spot(j, v, h)
        remote(here, here, send.at[0], mark(j, v, h), sibling, side).wait_recv()
        return here

    for h in range(2):
        own = own_ref.at[pl.ds(h * half, half)]
        other = own_ref.at[pl.ds((1 - h) * half, half)]
        for v in across:
            hand(own, member, side, h, me, v)
        hand(other, member, side, 1 - h, first + opposite, side)
    for h in range(2):
        hand(own_ref.at[pl.ds(h * half, half)], member, side, h, sibling, side)
    keep = [
        pltpu.make_async_copy(own_ref.at[pl.ds(h * half, half)], spot(member, side, h), local.at[h])
        for h in range(2)
    ]
    for copy in keep:
        copy.start()

    @pl.when(group == 0)
    def _():
        rows_ref[0] = jnp.zeros_like(rows_ref[0])

    @pl.when(group == groups - 1)
    def _():
        rows_ref[last] = jnp.zeros_like(rows_ref[last])

    for v in across:
        here = arrived(member, v, 0)
        hand(here, member, v, 0, first + opposite, side)
        hand(here, member, v, 0, sibling, side)
    here = arrived(opposite, side, 1)
    for v in across:
        hand(here, opposite, side, 1, me, v)
    hand(here, opposite, side, 1, sibling, side)
    for v in across:
        hand(arrived(member, v, 1), member, v, 1, sibling, side)
    hand(arrived(opposite, side, 0), opposite, side, 0, sibling, side)
    for v in across:
        for h in range(2):
            hand(arrived(opposite, v, h), opposite, v, h, sibling, side)
    for p in range(2):
        for v in range(sides):
            for h in range(2):
                arrived(p * 2 + 1 - core, v, h)

    @pl.when(group > 0)
    def _():
        for v in range(sides):
            remote(edge(0, v), edge(0, v), edge_send.at[0], edge_recv.at[v], sibling, side).wait_recv()

    @pl.when(group < groups - 1)
    def _():
        for v in range(sides):
            mark = edge_recv.at[sides + v]
            remote(edge(last, v), edge(last, v), edge_send.at[0], mark, sibling, side).wait_recv()

    for copy in keep:
        copy.wait()
    for copy in sent:
        copy.wait_send()

    @pl.when(sends_up)
    def _():
        for copy in edge_copies(True):
            copy.wait_send()

    @pl.when(sends_down)
    def _():
        for copy in edge_copies(False):
            copy.wait_send()


def group_rows(members, groups, sides, features):
    side_rows, width, channels = features.shape
    count = members * sides
    dma = pltpu.SemaphoreType.DMA
    return pl.pallas_call(
        functools.partial(gather_kernel, members, groups, sides),
        out_shape=jax.ShapeDtypeStruct(
            (members * side_rows + 2, sides * width, channels), features.dtype
        ),
        in_specs=[pl.BlockSpec(memory_space=pltpu.HBM)],
        out_specs=pl.BlockSpec(memory_space=pltpu.VMEM),
        scratch_shapes=[
            dma((4 * count,)),
            dma((2 * count,)),
            dma((2 * count,)),
            dma((2 * sides,)),
            dma((2,)),
        ],
        compiler_params=pltpu.CompilerParams(
            collective_id=0, has_side_effects=True, vmem_limit_bytes=16 * 2**20
        ),
        cost_estimate=pl.CostEstimate(flops=0, bytes_accessed=55 * 10**6, transcendentals=0),
    )(features)


def reduce_kernel(
    members,
    groups,
    step,
    share_ref,
    weights_ref,
    new_ref,
    old,
    near,
    relay,
    joined,
    far,
    fresh,
    near_send,
    near_recv,
    relay_send,
    relay_recv,
    far_send,
    far_recv,
    out_send,
    out_recv,
    local,
):
    me, side = lax.axis_index("space"), lax.axis_index("clus")
    group, member = me // members, me % members
    clusters, taps, depth, species = old.shape
    piece = depth // members
    pairs = groups // 2
    pair = group // 2

    def joint_of(p):
        return p * 2 + (p < pairs // 2).astype(jnp.int32)

    def at(g):
        return g * members + member

    partner = pair * 2 + 1 - group % 2
    is_joint = group == joint_of(pair)
    not_joint = group != joint_of(pair)

    kept_weights = pltpu.make_async_copy(
        weights_ref.at[
            pl.ds(member * clusters, clusters),
            :,
            pl.ds(pl.multiple_of(group * depth, depth), depth),
        ],
        old,
        local.at[clusters],
    )
    kept_weights.start()

    greet(at(partner), side)
    for q in range(1, pairs):
        greet(at(joint_of(lax.rem(pair + q, pairs))), side)
    for o in range(1, members):
        greet(group * members + lax.rem(member + o, members), side)
    pl.semaphore_wait(
        pltpu.get_barrier_semaphore(), members + is_joint.astype(jnp.int32) * (2 * (pairs - 1))
    )

    parts = [(c, q, e) for c in range(clusters) for q in range(1, pairs) for e in range(2)]

    def index(c, q, e):
        return (c * (pairs - 1) + q - 1) * 2 + e

    def to_partner(c):
        return remote(
            share_ref.at[partner, c], near.at[c], near_send.at[c], near_recv.at[c], at(partner), side
        )

    def to_joint(c, q, e):
        i = index(c, q, e)
        return remote(
            share_ref.at[lax.rem(pair + q, pairs) * 2 + e, c],
            relay.at[i],
            relay_send.at[i],
            relay_recv.at[i],
            at(partner),
            side,
        )

    def across(c, q, e):
        i = index(c, q, e)
        j = c * (pairs - 1) + q - 1
        to = lax.rem(pair + q, pairs) * 2 + e
        return remote(joined.at[i], far.at[j], far_send.at[i], far_recv.at[j], at(to), side)

    def handed(c, o):
        to = lax.rem(member + o, members)
        i = c * members + o
        return remote(
            fresh.at[to, c],
            new_ref.at[member * clusters + c],
            out_send.at[i],
            out_recv.at[i],
            group * members + to,
            side,
        )

    def kept(c):
        return pltpu.make_async_copy(
            fresh.at[member, c], new_ref.at[member * clusters + c], local.at[c]
        )

    @pl.when(not_joint)
    def _():
        for c, q, e in parts:
            to_joint(c, q, e).start()

    for c in range(clusters):
        to_partner(c).start()

    @pl.when(is_joint)
    def _():
        for c, q, e in parts:
            to_joint(c, q, e).wait_recv()
            i, to = index(c, q, e), lax.rem(pair + q, pairs) * 2 + e

            def join(tap, carry, i=i, to=to, c=c):
                total = share_ref[to, c, tap].astype(jnp.float32) + relay[i, tap].astype(jnp.float32)
                joined[i, tap] = total.astype(joined.dtype)
                return carry

            lax.fori_loop(0, taps, join, 0)
            across(c, q, e).start()

    kept_weights.wait()
    for c in range(clusters):
        to_partner(c).wait_recv()
        for q in range(1, pairs):
            across(c, q, 0).wait_recv()

        def one_tap(tap, carry, c=c):
            total = share_ref[group, c, tap].astype(jnp.float32) + near[c, tap].astype(jnp.float32)
            for q in range(1, pairs):
                total = total + far[c * (pairs - 1) + q - 1, tap].astype(jnp.float32)
            new = old[c, tap].astype(jnp.float32) - step * total
            fresh[:, c, tap] = new.reshape(members, piece, species).astype(fresh.dtype)
            return carry

        lax.fori_loop(0, taps, one_tap, 0)
        for o in range(1, members):
            handed(c, o).start()
        kept(c).start()
    for c in range(clusters):
        kept(c).wait()
        for o in range(1, members):
            handed(c, o).wait()
        to_partner(c).wait_send()

    @pl.when(not_joint)
    def _():
        for c, q, e in parts:
            to_joint(c, q, e).wait_send()

    @pl.when(is_joint)
    def _():
        for c, q, e in parts:
            across(c, q, e).wait_send()


def new_shares(members, step, share, weights):
    groups, clusters, taps, depth, species = share.shape
    away = clusters * (groups // 2 - 1)
    block = (taps, depth, species)
    dma = pltpu.SemaphoreType.DMA
    vmem = pl.BlockSpec(memory_space=pltpu.VMEM)
    return pl.pallas_call(
        functools.partial(reduce_kernel, members, groups, step),
        out_shape=jax.ShapeDtypeStruct(
            (members * clusters, taps, depth // members, species), weights.dtype
        ),
        in_specs=[vmem, pl.BlockSpec(memory_space=pltpu.HBM)],
        out_specs=vmem,
        scratch_shapes=[
            pltpu.VMEM((clusters,) + block, weights.dtype),
            pltpu.VMEM((clusters,) + block, share.dtype),
            pltpu.VMEM((2 * away,) + block, share.dtype),
            pltpu.VMEM((2 * away,) + block, share.dtype),
            pltpu.VMEM((away,) + block, share.dtype),
            pltpu.VMEM((members, clusters, taps, depth // members, species), weights.dtype),
            dma((clusters,)),
            dma((clusters,)),
            dma((2 * away,)),
            dma((2 * away,)),
            dma((2 * away,)),
            dma((away,)),
            dma((clusters * members,)),
            dma((clusters * members,)),
            dma((clusters + 1,)),
        ],
        compiler_params=pltpu.CompilerParams(
            collective_id=1, has_side_effects=True, vmem_limit_bytes=24 * 2**20
        ),
        cost_estimate=pl.CostEstimate(flops=10**6, bytes_accessed=4 * 10**6, transcendentals=0),
    )(share, weights)


def shards(members, sides, features, weights, tile_lists, labels):
    groups = lax.axis_size("space") // members
    channels = weights.shape[2]
    rows = group_rows(members, groups, sides, features)
    share = gradient_shares(members, groups, tile_lists, rows, weights, labels)
    step = math.sqrt(9 * channels * SIDE * SIDE / tile_lists.shape[1]) / math.sqrt(9 * channels)
    return new_shares(members, step, share, weights)


def solution(mesh):
    in_specs = (
        P("space", "clus", None),
        P("clus", None, None, None),
        P("clus", None),
        P("clus", None, None),
    )
    out_specs = P("clus", None, "space", None)
    members = 4
    return jax.shard_map(
        functools.partial(shards, members, mesh.shape["clus"]),
        mesh=mesh,
        in_specs=in_specs,
        out_specs=out_specs,
        check_vma=False,
    )
```
